256 devices in a mesh: pipe: 16 (over x_hi, z), seq: 2 (over x_lo), tensor: 8 (over y, core).
Axes of the slice: x: 4 (x_hi: 2, x_lo: 2; x = x_hi * 2 + x_lo), y: 4, z: 8, core: 2. Of those that a mesh axis runs over, the one named last changes fastest.
Arguments:
- ffn_input: bfloat16 [1024, 8192], P(None, ('seq', 'tensor')), may hold values from -6 to 6
- w_gate_up: bfloat16 [2, 8192, 14336], P(None, ('seq', 'tensor'), 'pipe'), may hold values from -0.0625 to 0.0625
- w_down: bfloat16 [14336, 8192], P('pipe', ('seq', 'tensor')), may hold values from -0.046875 to 0.046875
- stream: bfloat16 [1024, 8192], P('pipe', ('seq', 'tensor')), may hold values from -6 to 6
- attn_gain: float32 [8192], replicated, may hold values from 0.1 to 1.9
- w_query: bfloat16 [8192, 8, 4, 128], P(None, 'tensor', 'seq'), may hold values from -0.0625 to 0.0625
- w_kv: bfloat16 [8192, 2, 8, 128], P(None, None, 'tensor'), may hold values from -0.0625 to 0.0625
- cache_kv: bfloat16 [16, 2, 1024, 8, 128], P('pipe', None, None, 'tensor'), may hold values from -62 to 62
- cache_len: int32 [16], P('pipe'), may hold values from 1 to 1024, as said below
Outputs:
- stream_out: bfloat16 [1024, 8192], P('pipe', ('seq', 'tensor'))
- attended: bfloat16 [1024, 8, 4, 128], P('pipe', 'tensor', 'seq')
The draws below stay inside these ranges and needn't reach their ends.
Inputs may be any that keep to these rules, and one draw needn't show every extreme that they name: Each request's cache holds valid entries at its first cache_len positions; in every draw some request fills all 1024 positions.
All inputs are finite; a program needn't handle non-finite values.
Results may differ from the reference program's by a relative error of at most 0.034.
Values may be sent and summed in bfloat16 or wider, within the bound.
A program may use at most 128 MiB of HBM per device.

```python
import math
import jax
import jax.numpy as jnp
from jax import lax

D = 8192
HEAD = 128
KVH = 8
FF = 14336
GROUP = 4
SPAN = 64
CACHE = 1024
REQUESTS = 16
TOKENS = 1024


def draw_cache_kv(key, part):
    key = jax.random.fold_in(key, 11)
    full_shape = (REQUESTS, 2, CACHE, KVH, HEAD)
    return jnp.clip(jax.random.normal(key, full_shape, jnp.float32), -6.0, 6.0).astype(jnp.bfloat16)


def draw_cache_len(key, part):
    key = jax.random.fold_in(key, 5)
    lengths = jax.random.randint(key, (REQUESTS,), 1, CACHE + 1)
    chosen = jax.random.randint(jax.random.fold_in(key, 1), (), 0, REQUESTS)
    return jnp.where(jnp.arange(REQUESTS) == chosen, CACHE, lengths).astype(jnp.int32)


def shard_levels(stream_key, shape, shards, smallest, high):
    def one(axis_at, blocks):
        heights = jax.random.uniform(jax.random.fold_in(jax.random.fold_in(stream_key, 6), axis_at), (blocks,), jnp.float32, smallest / len(shards), high / len(shards))
        return jnp.repeat(jnp.exp(heights), shape[axis_at] // blocks).reshape((-1,) + (1,) * (len(shape) - axis_at - 1))

    level = one(*shards[0])
    for cut in shards[1:]:
        level = level * one(*cut)
    return level


def normal_values(key, dims, spread, bound, pieces=(), kind=jnp.bfloat16):
    drawn = jax.random.normal(key, dims, jnp.float32) * spread
    if len(pieces) > 0:
        drawn = shard_levels(key, dims, pieces, -0.22, 0.18) * drawn
    return jnp.clip(drawn, min=-bound, max=bound).astype(kind)


def setup_inputs(seed: int = 0) -> dict:
    keys = jax.random.split(jax.random.key(seed), 10)
    return {
        "ffn_input": normal_values(keys[0], (TOKENS, D), 1.0, 6.0, ((1, 16),)),
        "w_gate_up": normal_values(keys[1], (2, D, FF), D ** -0.5, 0.0625, ((1, 16), (2, 16))),
        "w_down": normal_values(keys[2], (FF, D), FF ** -0.5, 0.046875, ((0, 16), (1, 16))),
        "stream": normal_values(keys[3], (TOKENS, D), 1.0, 6.0, ((0, 16), (1, 16))),
        "attn_gain": jnp.clip(1.0 + 0.18 * jax.random.normal(keys[4], (D,), jnp.float32), 0.1, 1.9),
        "w_query": normal_values(keys[5], (D, KVH, GROUP, HEAD), D ** -0.5, 0.0625, ((1, 8), (2, 2))),
        "w_kv": normal_values(keys[6], (D, 2, KVH, HEAD), D ** -0.5, 0.0625, ((2, 8),)),
        "cache_kv": draw_cache_kv(jax.random.fold_in(keys[9], 71), 0),
        "cache_len": draw_cache_len(jax.random.fold_in(keys[9], 71), 0),
    }


norm_eps = 1e-05
rope_theta = 500000.0

def rotate(values, cosine, sine_part):
    half_dim = values.shape[-1] // 2
    first_half = values[..., :half_dim]
    second_half = values[..., half_dim:]
    return jnp.concatenate([first_half * cosine - second_half * sine_part, second_half * cosine + first_half * sine_part], axis=-1)

def attend(queries, new_keys, new_vals, cache_keys, cache_vals, cache_len):
    head_scale = queries.shape[-1] ** (-0.5)
    cache_count = cache_keys.shape[1]
    span_len = queries.shape[1]
    cache_scores = jnp.einsum('rckgh,rlkh->rkgcl', queries.astype(jnp.float32), cache_keys.astype(jnp.float32)) * head_scale
    own_scores = jnp.einsum('rckgh,rjkh->rkgcj', queries.astype(jnp.float32), new_keys.astype(jnp.float32)) * head_scale
    cache_valid = (jnp.arange(cache_count, dtype=jnp.int32)[None, :] < cache_len[:, None])[:, None, None, None, :]
    causal = (jnp.arange(span_len, dtype=jnp.int32)[None, :] <= jnp.arange(span_len, dtype=jnp.int32)[:, None])[None, None, None, :, :]
    cache_scores = jnp.where(cache_valid, cache_scores, -1e+30)
    own_scores = jnp.where(causal, own_scores, -1e+30)
    row_max = jnp.maximum(lax.optimization_barrier(jnp.max(cache_scores, axis=-1, keepdims=True)), lax.optimization_barrier(jnp.max(own_scores, axis=-1, keepdims=True)))
    cache_exp = jnp.exp(cache_scores - row_max)
    own_exp = jnp.exp(own_scores - row_max)
    denominator = lax.optimization_barrier(jnp.sum(cache_exp, axis=-1, keepdims=True)) + lax.optimization_barrier(jnp.sum(own_exp, axis=-1, keepdims=True))
    cache_w = (cache_exp / denominator).astype(jnp.bfloat16)
    own_w = (own_exp / denominator).astype(jnp.bfloat16)
    result = jnp.einsum('rkgcl,rlkh->rckgh', cache_w.astype(jnp.float32), cache_vals.astype(jnp.float32))
    result = result + jnp.einsum('rkgcj,rjkh->rckgh', own_w.astype(jnp.float32), new_vals.astype(jnp.float32))
    return result.astype(jnp.bfloat16)

def reference(ffn_input, w_gate_up, w_down, stream, attn_gain, w_query, w_kv, cache_kv, cache_len):
    gate = jnp.dot(ffn_input, w_gate_up[0], preferred_element_type=jnp.float32)
    up_part = jnp.dot(ffn_input, w_gate_up[1], preferred_element_type=jnp.float32)
    hidden = (jax.nn.silu(gate) * up_part).astype(jnp.bfloat16)
    ffn_out = jnp.dot(hidden, w_down, preferred_element_type=jnp.float32)
    mixed = (stream.astype(jnp.float32) + ffn_out).astype(jnp.bfloat16)
    wide = mixed.astype(jnp.float32)
    mean_sq = lax.optimization_barrier(jnp.mean(wide * wide, axis=1, keepdims=True))
    normed = (wide * lax.rsqrt(mean_sq + norm_eps) * attn_gain).astype(jnp.bfloat16)
    queries = jnp.dot(normed, w_query.reshape(D, KVH * GROUP * HEAD), preferred_element_type=jnp.float32).reshape(TOKENS, KVH, GROUP, HEAD)
    keyval = jnp.dot(normed, w_kv.reshape(D, 2 * KVH * HEAD), preferred_element_type=jnp.float32).reshape(TOKENS, 2, KVH, HEAD)
    half_dim = HEAD // 2
    positions = (cache_len[:, None] + jnp.arange(SPAN, dtype=jnp.int32)[None, :]).reshape(TOKENS).astype(jnp.float32)
    inv_freq = jnp.exp(jnp.arange(half_dim, dtype=jnp.float32) * (-2.0 * math.log(rope_theta) / HEAD))
    angles = positions[:, None] * inv_freq[None, :]
    cosine = jnp.cos(angles)
    sine_part = jnp.sin(angles)
    q_rot = rotate(queries, cosine[:, None, None, :], sine_part[:, None, None, :]).astype(jnp.bfloat16)
    k_new = rotate(keyval[:, 0], cosine[:, None, :], sine_part[:, None, :]).astype(jnp.bfloat16)
    v_new = keyval[:, 1].astype(jnp.bfloat16)
    q_rot = q_rot.reshape(REQUESTS, SPAN, KVH, GROUP, HEAD)
    k_new = k_new.reshape(REQUESTS, SPAN, KVH, HEAD)
    v_new = v_new.reshape(REQUESTS, SPAN, KVH, HEAD)
    attended = attend(q_rot, k_new, v_new, cache_kv[:, 0], cache_kv[:, 1], cache_len)
    return (mixed, attended.reshape(TOKENS, KVH, GROUP, HEAD))
```

```python
import math

import jax
import jax.numpy as jnp
from jax import lax
from jax.experimental import pallas as pl
from jax.experimental.pallas import tpu as pltpu
from jax.sharding import PartitionSpec as P

norm_eps = 1e-05
rope_theta = 500000.0
MESH = pl.DeviceIdType.MESH
BF = jnp.bfloat16
F32 = jnp.float32

CHUNKS = 4
ROWS = 16
CHIPS = 8
OFFSETS = [(a, b) for a in range(2) for b in range(4)][1:]


def rotate(values, cosine, sine_part):
    half_dim = values.shape[-1] // 2
    first_half = values[..., :half_dim]
    second_half = values[..., half_dim:]
    return jnp.concatenate(
        [
            first_half * cosine - second_half * sine_part,
            second_half * cosine + first_half * sine_part,
        ],
        axis=-1,
    )


def attend(queries, new_keys, new_vals, cache_keys, cache_vals, cache_len):
    head_scale = queries.shape[-1] ** (-0.5)
    cache_count = cache_keys.shape[1]
    span_len = queries.shape[1]
    cache_scores = (
        jnp.einsum("rckgh,rlkh->rkgcl", queries, cache_keys, preferred_element_type=jnp.float32)
        * head_scale
    )
    own_scores = (
        jnp.einsum("rckgh,rjkh->rkgcj", queries, new_keys, preferred_element_type=jnp.float32)
        * head_scale
    )
    cache_valid = (jnp.arange(cache_count, dtype=jnp.int32)[None, :] < cache_len[:, None])[
        :, None, None, None, :
    ]
    causal = (
        jnp.arange(span_len, dtype=jnp.int32)[None, :]
        <= jnp.arange(span_len, dtype=jnp.int32)[:, None]
    )[None, None, None, :, :]
    cache_scores = jnp.where(cache_valid, cache_scores, -1e30)
    own_scores = jnp.where(causal, own_scores, -1e30)
    row_max = jnp.maximum(
        jnp.max(cache_scores, axis=-1, keepdims=True), jnp.max(own_scores, axis=-1, keepdims=True)
    )
    cache_exp = jnp.exp(cache_scores - row_max)
    own_exp = jnp.exp(own_scores - row_max)
    denominator = jnp.sum(cache_exp, axis=-1, keepdims=True) + jnp.sum(
        own_exp, axis=-1, keepdims=True
    )
    cache_w = (cache_exp / denominator).astype(jnp.bfloat16)
    own_w = (own_exp / denominator).astype(jnp.bfloat16)
    result = jnp.einsum(
        "rkgcl,rlkh->rckgh", cache_w, cache_vals, preferred_element_type=jnp.float32
    )
    result = result + jnp.einsum(
        "rkgcj,rjkh->rckgh", own_w, new_vals, preferred_element_type=jnp.float32
    )
    return result.astype(jnp.bfloat16)


def wait_bytes(ref, sem):
    pltpu.make_async_copy(ref, ref, sem).wait()


def ffn_kernel(
    x_hbm,
    wgu_hbm,
    wd_hbm,
    stream_ref,
    mixed_ref,
    full_ref,
    x_v,
    wgu_v,
    wd_v,
    core_send,
    core_recv,
    rs_send,
    rs_recv,
    hid_own,
    hid_all,
    z_send,
    z_recv,
    xh_send,
    xh_recv,
    xh_own,
    full_all,
    load_sem,
    send_sem,
    recv_sem,
):
    p = lax.axis_index("pipe")
    s = lax.axis_index("seq")
    t = lax.axis_index("tensor")
    xh, z = p // 8, p % 8
    y, core = t // 2, t % 2
    k = s * 4 + y
    sibling = (p, s, y * 2 + 1 - core)

    loads = [
        pltpu.make_async_copy(src, dst, load_sem.at[i])
        for i, (src, dst) in enumerate(((x_hbm, x_v), (wgu_hbm, wgu_v), (wd_hbm, wd_v)))
    ]
    for load in loads:
        load.start()

    def group_peer(da, db):
        s2 = (s + da) % 2
        y2 = (y + db) % 4
        return s2 * 4 + y2, (p, s2, y2 * 2 + core)

    def z_peer(dz):
        z2 = (z + dz) % 8
        return z2, (xh * 8 + z2, s, t)

    x_peer = ((1 - xh) * 8 + z, s, t)

    barrier = pltpu.get_barrier_semaphore()
    everyone = [sibling, x_peer]
    everyone += [group_peer(*o)[1] for o in OFFSETS]
    everyone += [z_peer(dz)[1] for dz in range(1, 8)]
    for peer in everyone:
        pl.semaphore_signal(barrier, inc=1, device_id=peer, device_id_type=MESH)

    def send(src, dst, kind, c, peer):
        pltpu.make_async_remote_copy(
            src_ref=src,
            dst_ref=dst,
            send_sem=send_sem.at[kind, c],
            recv_sem=recv_sem.at[kind, c],
            device_id=peer,
            device_id_type=MESH,
        ).start()

    def gate_up(rows, c):
        left = x_v[:, rows, pl.ds(c * ROWS, ROWS), :].reshape(CHIPS * ROWS, 512)
        return [
            jnp.dot(left, wgu_v[e], preferred_element_type=F32).reshape(CHIPS, ROWS, 896)
            for e in range(2)
        ]

    def stage_a(c):
        for e, part in enumerate(gate_up(1 - core, c)):
            core_send[c, :, :, e * 896 : (e + 1) * 896] = part.astype(BF)
        send(core_send.at[c], core_recv.at[c], 0, c, sibling)

    def stage_b(c):
        parts = gate_up(core, c)
        wait_bytes(core_recv.at[c], recv_sem.at[0, c])
        for e, part in enumerate(parts):
            cols = slice(e * 896, (e + 1) * 896)
            rs_send[c, :, :, cols] = (part + core_recv[c, :, :, cols].astype(F32)).astype(BF)
        for j, o in enumerate(OFFSETS):
            k2, peer = group_peer(*o)
            send(rs_send.at[c, k2], rs_recv.at[c, j], 1, c, peer)

    def stage_c(c):
        wait_bytes(rs_recv.at[c], recv_sem.at[1, c])
        total = rs_send[c, k].astype(F32)
        for j in range(7):
            total = total + rs_recv[c, j].astype(F32)
        gate, up = total[:, :896], total[:, 896:]
        hidden = (jax.nn.silu(gate) * up).astype(BF)
        hid_own[c] = hidden
        hid_all[c, k, core] = hidden
        for o in OFFSETS:
            _, peer = group_peer(*o)
            send(hid_own.at[c], hid_all.at[c, k, core], 2, c, peer)

    def stage_d(c):
        wait_bytes(hid_all.at[c, 0:7, 0], recv_sem.at[2, c])
        send(hid_all.at[c, :, core], hid_all.at[c, :, core], 3, c, sibling)

    def stage_e(c):
        wait_bytes(hid_all.at[c, :, 0], recv_sem.at[3, c])
        left = hid_all[c].reshape(2 * CHIPS * ROWS, 896)
        z_send[c] = (
            jnp.dot(left, wd_v[...], preferred_element_type=F32).astype(BF).reshape(2, 8, ROWS, 512)
        )
        for dz in range(1, 8):
            z2, peer = z_peer(dz)
            send(z_send.at[c, :, z2], z_recv.at[c, dz - 1], 4, c, peer)

    def stage_f(c):
        wait_bytes(z_recv.at[c], recv_sem.at[4, c])

        def total(a):
            value = z_send[c, a, z].astype(F32)
            for j in range(7):
                value = value + z_recv[c, j, a].astype(F32)
            return value

        xh_send[c] = total(1 - xh).astype(BF)
        send(xh_send.at[c], xh_recv.at[c], 5, c, x_peer)
        xh_own[c] = total(xh)

    def stage_g(c):
        wait_bytes(xh_recv.at[c], recv_sem.at[5, c])
        rows = slice(c * ROWS, (c + 1) * ROWS)
        ffn_out = xh_own[c] + xh_recv[c].astype(F32)
        mixed = (stream_ref[rows, :].astype(F32) + ffn_out).astype(BF)
        mixed_ref[rows, :] = mixed
        full_all[c, k, core] = mixed
        for o in OFFSETS:
            _, peer = group_peer(*o)
            send(mixed_ref.at[rows], full_all.at[c, k, core], 6, c, peer)

    def stage_h(c):
        wait_bytes(full_all.at[c, 0:7, 0], recv_sem.at[6, c])
        send(full_all.at[c, :, core], full_all.at[c, :, core], 7, c, sibling)

    def stage_i(c):
        wait_bytes(full_all.at[c, :, 0], recv_sem.at[7, c])
        rows = slice(c * ROWS, (c + 1) * ROWS)
        for m in range(16):
            full_ref[rows, m * 512 : (m + 1) * 512] = full_all[c, m // 2, m % 2]

    loads[0].wait()
    loads[1].wait()
    pl.semaphore_wait(barrier, len(everyone))
    stages = dict(
        a=stage_a, b=stage_b, c=stage_c, d=stage_d, e=stage_e, f=stage_f, g=stage_g, h=stage_h, i=stage_i
    )
    order = (
        "a0", "a1", "b0", "a2", "b1", "a3", "b2", "b3", "c0",
        "c1", "d0", "c2", "d1", "e0", "c3", "d2", "e1", "f0",
        "d3", "e2", "f1", "g0", "e3", "f2", "g1", "h0", "f3",
        "g2", "h1", "i0", "g3", "h2", "i1", "h3", "i2", "i3",
    )
    waited = False
    for step in order:
        if step[0] == "e" and not waited:
            loads[2].wait()
            waited = True
        stages[step[0]](int(step[1]))

    for c in range(CHUNKS):
        wait_bytes(core_send.at[c], send_sem.at[0, c])
        wait_bytes(rs_recv.at[c], send_sem.at[1, c])
        wait_bytes(hid_all.at[c, 0:7, 0], send_sem.at[2, c])
        wait_bytes(hid_all.at[c, :, 0], send_sem.at[3, c])
        wait_bytes(z_recv.at[c], send_sem.at[4, c])
        wait_bytes(xh_send.at[c], send_sem.at[5, c])
        wait_bytes(full_all.at[c, 0:7, 0], send_sem.at[6, c])
        wait_bytes(full_all.at[c, :, 0], send_sem.at[7, c])


def ffn_block(ffn_input, w_gate_up, w_down, stream):
    vmem = pl.BlockSpec(memory_space=pltpu.VMEM)
    hbm = pl.BlockSpec(memory_space=pl.ANY)
    return pl.pallas_call(
        ffn_kernel,
        out_shape=(
            jax.ShapeDtypeStruct((64, 512), BF),
            jax.ShapeDtypeStruct((64, 8192), BF),
        ),
        in_specs=[hbm, hbm, hbm, vmem],
        out_specs=(vmem, vmem),
        scratch_shapes=[
            pltpu.VMEM((CHIPS, 2, 64, 512), BF),
            pltpu.VMEM((2, 512, 896), BF),
            pltpu.VMEM((896, 512), BF),
            pltpu.VMEM((CHUNKS, CHIPS, ROWS, 1792), BF),
            pltpu.VMEM((CHUNKS, CHIPS, ROWS, 1792), BF),
            pltpu.VMEM((CHUNKS, CHIPS, ROWS, 1792), BF),
            pltpu.VMEM((CHUNKS, 7, ROWS, 1792), BF),
            pltpu.VMEM((CHUNKS, ROWS, 896), BF),
            pltpu.VMEM((CHUNKS, CHIPS, 2, ROWS, 896), BF),
            pltpu.VMEM((CHUNKS, 2, 8, ROWS, 512), BF),
            pltpu.VMEM((CHUNKS, 7, 2, ROWS, 512), BF),
            pltpu.VMEM((CHUNKS, ROWS, 512), BF),
            pltpu.VMEM((CHUNKS, ROWS, 512), BF),
            pltpu.VMEM((CHUNKS, ROWS, 512), F32),
            pltpu.VMEM((CHUNKS, CHIPS, 2, ROWS, 512), BF),
            pltpu.SemaphoreType.DMA((3,)),
            pltpu.SemaphoreType.DMA((8, CHUNKS)),
            pltpu.SemaphoreType.DMA((8, CHUNKS)),
        ],
        compiler_params=pltpu.CompilerParams(
            collective_id=0, has_side_effects=True, vmem_limit_bytes=36 * 1024 * 1024
        ),
        name="ffn_block",
    )(ffn_input.reshape(CHIPS, 2, 64, 512), w_gate_up, w_down, stream)


def body(ffn_input, w_gate_up, w_down, stream, attn_gain, w_query, w_kv, cache_kv, cache_len):
    group_rows = stream.shape[0]
    mixed, full_rows = ffn_block(ffn_input, w_gate_up, w_down, stream)
    wide = full_rows.astype(jnp.float32)
    mean_sq = jnp.mean(wide * wide, axis=1, keepdims=True)
    normed = (wide * lax.rsqrt(mean_sq + norm_eps) * attn_gain).astype(jnp.bfloat16)
    queries = jnp.einsum("td,dkgh->tkgh", normed, w_query, preferred_element_type=jnp.float32)
    keyval = jnp.einsum("td,dekh->tekh", normed, w_kv, preferred_element_type=jnp.float32)
    requests = cache_len.shape[0]
    span_len = group_rows // requests
    head_dim = w_query.shape[3]
    half_dim = head_dim // 2
    positions = (
        (cache_len[:, None] + jnp.arange(span_len, dtype=jnp.int32)[None, :])
        .reshape(group_rows)
        .astype(jnp.float32)
    )
    inv_freq = jnp.exp(
        jnp.arange(half_dim, dtype=jnp.float32) * (-2.0 * math.log(rope_theta) / head_dim)
    )
    angles = positions[:, None] * inv_freq[None, :]
    cosine = jnp.cos(angles)
    sine_part = jnp.sin(angles)
    q_rot = rotate(queries, cosine[:, None, None, :], sine_part[:, None, None, :]).astype(
        jnp.bfloat16
    )
    k_new = rotate(keyval[:, 0], cosine[:, None, :], sine_part[:, None, :]).astype(jnp.bfloat16)
    v_new = keyval[:, 1].astype(jnp.bfloat16)
    kv_local = w_query.shape[1]
    group_local = w_query.shape[2]
    q_rot = q_rot.reshape(requests, span_len, kv_local, group_local, head_dim)
    k_new = k_new.reshape(requests, span_len, kv_local, head_dim)
    v_new = v_new.reshape(requests, span_len, kv_local, head_dim)
    attended = attend(q_rot, k_new, v_new, cache_kv[:, 0], cache_kv[:, 1], cache_len)
    return (mixed, attended.reshape(group_rows, kv_local, group_local, head_dim))


def solution(mesh):
    in_specs = (
        P(None, ("seq", "tensor")),
        P(None, ("seq", "tensor"), "pipe"),
        P("pipe", ("seq", "tensor")),
        P("pipe", ("seq", "tensor")),
        P(),
        P(None, "tensor", "seq", None),
        P(None, None, "tensor", None),
        P("pipe", None, None, "tensor", None),
        P("pipe"),
    )
    out_specs = (P("pipe", ("seq", "tensor")), P("pipe", "tensor", "seq", None))
    return jax.shard_map(body, mesh=mesh, in_specs=in_specs, out_specs=out_specs, check_vma=False)
```

```python
import math

import jax
import jax.numpy as jnp
from jax import lax
from jax.experimental import pallas as pl
from jax.experimental.pallas import tpu as pltpu
from jax.sharding import PartitionSpec as P

norm_eps = 1e-05
rope_theta = 500000.0
MESH = pl.DeviceIdType.MESH
BF = jnp.bfloat16
F32 = jnp.float32

CHUNKS = 4
ROWS = 16
CHIPS = 8
OFFSETS = [(a, b) for a in range(2) for b in range(4)][1:]
WA, WB = 512, 384
KINDS = 19
(CORE, A1, B1, A2, B2, AY, AX, AR, BX, BY, BR, FA, FB, Z, ZH, ZF, XH, G, GF) = range(KINDS)
ORDER = (
    "a0", "a1", "b0", "a2", "b1", "r0", "a3", "b2", "c0", "b3", "w0",
    "c1", "j0", "w1", "c2", "j1", "w2", "d0", "c3", "j2", "w3", "d1",
    "k0", "j3", "e0", "w4", "d2", "k1", "e1", "w5", "d3", "k2", "q0",
    "e2", "w6", "k3", "q1", "e3", "w7", "g0", "q2", "g1", "q3", "h0",
    "g2", "i0", "h1", "g3", "i1", "h2", "i2", "h3", "i3", "t0",
)


def wait_bytes(ref, sem):
    pltpu.make_async_copy(ref, ref, sem).wait()


def ffn_kernel(
    x_hbm,
    wgu_hbm,
    wd_hbm,
    stream_ref,
    gain_ref,
    wq_hbm,
    wkv_hbm,
    cache_hbm,
    len_ref,
    mixed_ref,
    attended_ref,
    x_v,
    wgu_v,
    wd_v,
    core_send,
    core_recv,
    a_send,
    b_send,
    a_recv,
    b_recv,
    a_send2,
    a_recv2,
    b_own2,
    b_send2,
    b_recv2,
    hid_own,
    hid_a,
    hid_b,
    z_send,
    z_recv,
    zh_recv,
    zf_send,
    zf_recv,
    xh_recv,
    full_all,
    wq_v,
    wkv_v,
    cache_v,
    wide_w,
    spread,
    w_all,
    normed,
    cosine,
    sine,
    load_sem,
    send_sem,
    recv_sem,
):
    p = lax.axis_index("pipe")
    s = lax.axis_index("seq")
    t = lax.axis_index("tensor")
    xh, z = p // 8, p % 8
    y, core = t // 2, t % 2
    sibling = (p, s, y * 2 + 1 - core)
    seq_peer = (p, 1 - s, t)
    x_peer = ((1 - xh) * 8 + z, s, t)

    loads = [
        pltpu.make_async_copy(src, dst, load_sem.at[i])
        for i, (src, dst) in enumerate(
            (
                (x_hbm, x_v),
                (wgu_hbm, wgu_v),
                (wd_hbm, wd_v),
                (wq_hbm, wq_v),
                (wkv_hbm, wkv_v),
                (cache_hbm, cache_v),
            )
        )
    ]
    loads[0].start()
    loads[1].start()

    def y_peer(dy):
        y2 = (y + dy) % 4
        return y2, (p, s, y2 * 2 + core)

    def group_peer(da, dy):
        return (p, (s + da) % 2, (y + dy) % 4 * 2 + core)

    def z_peer(dz):
        z2 = (z + dz) % 8
        return z2, (xh * 8 + z2, s, t)

    def cross_peer(dz):
        return ((1 - xh) * 8 + (z + dz) % 8, s, t)

    barrier = pltpu.get_barrier_semaphore()
    everyone = [sibling, x_peer]
    everyone += [group_peer(*o) for o in OFFSETS]
    everyone += [z_peer(dz)[1] for dz in (1, 2, 3, 5, 6, 7)]
    everyone += [cross_peer(sign) for sign in (1, -1)]
    for peer in everyone:
        pl.semaphore_signal(barrier, inc=1, device_id=peer, device_id_type=MESH)

    def send(src, dst, kind, c, peer):
        pltpu.make_async_remote_copy(
            src_ref=src,
            dst_ref=dst,
            send_sem=send_sem.at[kind, c],
            recv_sem=recv_sem.at[kind, c],
            device_id=peer,
            device_id_type=MESH,
        ).start()

    def arrivals(kind, c):
        return {
            CORE: core_recv.at[c],
            A1: a_recv.at[c],
            B1: b_recv.at[c],
            A2: a_recv2.at[c],
            B2: b_recv2.at[c],
            AY: hid_a.at[c, 0, 0:3, 0],
            AX: hid_a.at[c, 0, 0, 0],
            AR: hid_a.at[c, 0, 0:3, 0],
            BX: hid_b.at[c, 0, 0, 0],
            BY: hid_b.at[c, 0, 0:3, 0],
            BR: hid_b.at[c, 0, 0:3, 0],
            FA: hid_a.at[c, :, :, 0],
            FB: hid_b.at[c, :, :, 0],
            Z: z_recv.at[c],
            ZH: zh_recv.at[c],
            ZF: zf_recv.at[c],
            XH: xh_recv.at[c],
            G: full_all.at[c, 0:7, 0],
            GF: full_all.at[c, :, 0],
        }[kind]

    def arrived(kind, c):
        wait_bytes(arrivals(kind, c), recv_sem.at[kind, c])

    def sent(kind, c):
        wait_bytes(arrivals(kind, c), send_sem.at[kind, c])

    def gate_up(rows, c):
        left = x_v[:, rows, pl.ds(c * ROWS, ROWS), :].reshape(CHIPS * ROWS, 512)
        return [
            jnp.dot(left, wgu_v[e], preferred_element_type=F32).reshape(CHIPS, ROWS, 896)
            for e in range(2)
        ]

    def stage_a(c):
        for e, part in enumerate(gate_up(1 - core, c)):
            core_send[c, :, :, e * 896 : (e + 1) * 896] = part.astype(BF)
        send(core_send.at[c], core_recv.at[c], CORE, c, sibling)

    def stage_b(c):
        parts = gate_up(core, c)
        arrived(CORE, c)
        for e, part in enumerate(parts):
            total = part + core_recv[c, :, :, e * 896 : (e + 1) * 896].astype(F32)
            total = total.astype(BF).reshape(2, 4, ROWS, 896)
            a_send[c, :, :, :, e * WA : (e + 1) * WA] = total[..., :WA]
            b_send[c, :, :, :, e * WB : (e + 1) * WB] = total[..., WA:]
        send(a_send.at[c, 1 - s], a_recv.at[c], A1, c, seq_peer)
        for dy in range(1, 4):
            y2, peer = y_peer(dy)
            send(b_send.at[c, :, y2], b_recv.at[c, dy - 1], B1, c, peer)

    def stage_c(c):
        arrived(A1, c)
        a_send2[c] = (a_send[c, s].astype(F32) + a_recv[c].astype(F32)).astype(BF)
        for dy in range(1, 4):
            y2, peer = y_peer(dy)
            send(a_send2.at[c, y2], a_recv2.at[c, dy - 1], A2, c, peer)
        arrived(B1, c)

        def total(a):
            value = b_send[c, a, y].astype(F32)
            for j in range(3):
                value = value + b_recv[c, j, a].astype(F32)
            return value

        b_send2[c] = total(1 - s).astype(BF)
        send(b_send2.at[c], b_recv2.at[c], B2, c, seq_peer)
        b_own2[c] = total(s)

    def stage_j(c):
        def swiglu(total, width):
            return (jax.nn.silu(total[:, :width]) * total[:, width:]).astype(BF)

        arrived(A2, c)
        total = a_send2[c, y].astype(F32)
        for j in range(3):
            total = total + a_recv2[c, j].astype(F32)
        hidden = swiglu(total, WA)
        hid_own[c, :, :WA] = hidden
        hid_a[c, s, y, core] = hidden
        own = hid_own.at[c, :, 0:WA]
        for dy in range(1, 4):
            send(own, hid_a.at[c, s, y, core], AY, c, y_peer(dy)[1])
        send(own, hid_a.at[c, s, y, core], AX, c, seq_peer)
        arrived(B2, c)
        hidden = swiglu(b_own2[c] + b_recv2[c].astype(F32), WB)
        hid_own[c, :, WA:] = hidden
        hid_b[c, s, y, core] = hidden
        own = hid_own.at[c, :, WA : WA + WB]
        send(own, hid_b.at[c, s, y, core], BX, c, seq_peer)
        for dy in range(1, 4):
            send(own, hid_b.at[c, s, y, core], BY, c, y_peer(dy)[1])

    def stage_d(c):
        arrived(AY, c)
        for dy in range(1, 4):
            y2, _ = y_peer(dy)
            send(hid_a.at[c, s, y2, core], hid_a.at[c, s, y2, core], AR, c, seq_peer)
        arrived(BX, c)
        for dy in range(1, 4):
            block = hid_b.at[c, 1 - s, y, core]
            send(block, block, BR, c, y_peer(dy)[1])

    def stage_k(c):
        arrived(AX, c)
        arrived(AR, c)
        send(hid_a.at[c, :, :, core], hid_a.at[c, :, :, core], FA, c, sibling)
        arrived(BY, c)
        arrived(BR, c)
        send(hid_b.at[c, :, :, core], hid_b.at[c, :, :, core], FB, c, sibling)

    def stage_e(c):
        arrived(FA, c)
        arrived(FB, c)
        out = jnp.dot(
            hid_a[c].reshape(256, WA), wd_v[:WA, :], preferred_element_type=F32
        ) + jnp.dot(hid_b[c].reshape(256, WB), wd_v[WA:, :], preferred_element_type=F32)
        z_send[c] = out.astype(BF).reshape(2, 8, ROWS, 512)
        send(z_send.at[c, 1 - xh, z], xh_recv.at[c], XH, c, x_peer)
        for way, sign in enumerate((1, -1)):
            for hop in (1, 2):
                z2, _ = z_peer(sign * (hop + 1))
                _, peer = z_peer(sign * hop)
                send(z_send.at[c, :, z2], z_recv.at[c, way, hop - 1], Z, c, peer)
            z2, _ = z_peer(4)
            _, peer = z_peer(sign * 3)
            half = pl.ds(way * 256, 256)
            send(z_send.at[c, :, z2, :, half], zh_recv.at[c, way], ZH, c, peer)

    def stage_q(c):
        arrived(Z, c)
        arrived(ZH, c)
        for way, sign in enumerate((1, -1)):
            z2, peer = z_peer(sign)
            for h in range(2):
                cols = slice(h * 256, (h + 1) * 256)
                total = z_send[c, :, z2, :, cols].astype(F32)
                for hop in range(2):
                    total = total + z_recv[c, way, hop, :, :, cols].astype(F32)
                if h == way:
                    total = total + zh_recv[c, way].astype(F32)
                zf_send[c, way, :, :, cols] = total.astype(BF)
            send(zf_send.at[c, way, xh], zf_recv.at[c, way, 0], ZF, c, peer)
            send(zf_send.at[c, way, 1 - xh], zf_recv.at[c, way, 1], ZF, c, cross_peer(sign))

    def stage_g(c):
        arrived(XH, c)
        arrived(ZF, c)
        rows = slice(c * ROWS, (c + 1) * ROWS)
        ffn_out = z_send[c, xh, z].astype(F32) + xh_recv[c].astype(F32)
        for way in range(2):
            for side in range(2):
                ffn_out = ffn_out + zf_recv[c, way, side].astype(F32)
        mixed = (stream_ref[rows, :].astype(F32) + ffn_out).astype(BF)
        mixed_ref[rows, :] = mixed
        full_all[c, s * 4 + y, core] = mixed
        for o in OFFSETS:
            send(mixed_ref.at[rows], full_all.at[c, s * 4 + y, core], G, c, group_peer(*o))

    def stage_h(c):
        arrived(G, c)
        send(full_all.at[c, :, core], full_all.at[c, :, core], GF, c, sibling)

    def stage_i(c):
        arrived(GF, c)
        rows = slice(c * ROWS, (c + 1) * ROWS)
        squares = jnp.zeros((ROWS, 1), F32)
        for m in range(16):
            wide = full_all[c, m // 2, m % 2].astype(F32)
            squares = squares + jnp.sum(wide * wide, axis=1, keepdims=True)
        scale = lax.rsqrt(squares * (1.0 / 8192) + norm_eps)
        for m in range(16):
            cols = slice(m * 512, (m + 1) * 512)
            wide = full_all[c, m // 2, m % 2].astype(F32)
            normed[rows, cols] = (wide * scale * gain_ref[:, cols]).astype(BF)

    def stage_w(n):
        if n == 0:
            loads[3].wait()
            loads[4].wait()
        for which, source in enumerate((wq_v, wkv_v)):
            for part in range(2):
                at = n * 1024 + part * 512
                wide_w[...] = source[2 * at : 2 * at + 1024, :].astype(F32)
                for e in range(2):
                    cols = slice((2 * which + e) * 128, (2 * which + e + 1) * 128)
                    w_all[at : at + 512, cols] = wide_w[pl.ds(e, 512, stride=2), :].astype(BF)

    def stage_r(_):
        lane = lax.broadcasted_iota(jnp.int32, (64, 128), 1)
        half = lax.rem(lane, 64)
        inv_freq = jnp.exp(half.astype(F32) * (-2.0 * math.log(rope_theta) / 128))
        row = lax.broadcasted_iota(jnp.int32, (64, 128), 0)
        angles = (len_ref[0] + row).astype(F32) * inv_freq
        cosine[...] = jnp.cos(angles)
        sine[...] = jnp.where(lane < 64, -1.0, 1.0) * jnp.sin(angles)

    def stage_t(_):
        def step(i, total):
            cols = pl.ds(pl.multiple_of(i * 1024, 1024), 1024)
            return total + jnp.dot(
                normed[:, cols], w_all[cols, :], preferred_element_type=F32
            )

        total = lax.fori_loop(0, 8, step, jnp.zeros((64, 512), F32))

        def rotated(value):
            return (value * cosine[...] + pltpu.roll(value, 64, 1) * sine[...]).astype(BF)

        queries = jnp.concatenate([rotated(total[:, :128]), rotated(total[:, 128:256])], axis=0)
        k_new = rotated(total[:, 256:384])
        v_new = total[:, 384:].astype(BF)
        loads[5].wait()
        head_scale = 128 ** (-0.5)
        dims = (((1,), (1,)), ((), ()))
        cache_scores = (
            lax.dot_general(queries, cache_v[0], dims, preferred_element_type=F32) * head_scale
        )
        own_scores = lax.dot_general(queries, k_new, dims, preferred_element_type=F32) * head_scale
        spot = lax.broadcasted_iota(jnp.int32, (128, 1024), 1)
        cache_scores = jnp.where(spot < len_ref[0], cache_scores, -1e30)
        row = lax.rem(lax.broadcasted_iota(jnp.int32, (128, 64), 0), 64)
        spot = lax.broadcasted_iota(jnp.int32, (128, 64), 1)
        own_scores = jnp.where(spot <= row, own_scores, -1e30)
        row_max = jnp.maximum(
            jnp.max(cache_scores, axis=1, keepdims=True), jnp.max(own_scores, axis=1, keepdims=True)
        )
        cache_exp = jnp.exp(cache_scores - row_max)
        own_exp = jnp.exp(own_scores - row_max)
        denominator = jnp.sum(cache_exp, axis=1, keepdims=True) + jnp.sum(
            own_exp, axis=1, keepdims=True
        )
        cache_w = (cache_exp / denominator).astype(BF)
        own_w = (own_exp / denominator).astype(BF)
        result = jnp.dot(cache_w, cache_v[1], preferred_element_type=F32)
        result = result + jnp.dot(own_w, v_new, preferred_element_type=F32)
        for g in range(2):
            spread[pl.ds(g, 64, stride=2), :] = result[g * 64 : (g + 1) * 64]
        attended_ref[...] = spread[...].astype(BF)

    loads[0].wait()
    loads[1].wait()
    for load in loads[2:]:
        load.start()
    pl.semaphore_wait(barrier, len(everyone))
    stages = dict(
        a=stage_a,
        b=stage_b,
        c=stage_c,
        j=stage_j,
        d=stage_d,
        k=stage_k,
        e=stage_e,
        q=stage_q,
        g=stage_g,
        h=stage_h,
        i=stage_i,
        w=stage_w,
        r=stage_r,
        t=stage_t,
    )
    waited = False
    for step in ORDER:
        if step[0] == "e" and not waited:
            loads[2].wait()
            waited = True
        stages[step[0]](int(step[1]))

    for c in range(CHUNKS):
        for kind in range(KINDS):
            sent(kind, c)


def ffn_block(ffn_input, w_gate_up, w_down, stream, attn_gain, w_query, w_kv, cache_kv, cache_len):
    vmem = pl.BlockSpec(memory_space=pltpu.VMEM)
    hbm = pl.BlockSpec(memory_space=pl.ANY)
    smem = pl.BlockSpec(memory_space=pltpu.SMEM)
    mixed, attended = pl.pallas_call(
        ffn_kernel,
        out_shape=(
            jax.ShapeDtypeStruct((64, 512), BF),
            jax.ShapeDtypeStruct((128, 128), BF),
        ),
        in_specs=[hbm, hbm, hbm, vmem, vmem, hbm, hbm, hbm, smem],
        out_specs=(vmem, vmem),
        scratch_shapes=[
            pltpu.VMEM((CHIPS, 2, 64, 512), BF),
            pltpu.VMEM((2, 512, 896), BF),
            pltpu.VMEM((896, 512), BF),
            pltpu.VMEM((CHUNKS, CHIPS, ROWS, 1792), BF),
            pltpu.VMEM((CHUNKS, CHIPS, ROWS, 1792), BF),
            pltpu.VMEM((CHUNKS, 2, 4, ROWS, 2 * WA), BF),
            pltpu.VMEM((CHUNKS, 2, 4, ROWS, 2 * WB), BF),
            pltpu.VMEM((CHUNKS, 4, ROWS, 2 * WA), BF),
            pltpu.VMEM((CHUNKS, 3, 2, ROWS, 2 * WB), BF),
            pltpu.VMEM((CHUNKS, 4, ROWS, 2 * WA), BF),
            pltpu.VMEM((CHUNKS, 3, ROWS, 2 * WA), BF),
            pltpu.VMEM((CHUNKS, ROWS, 2 * WB), F32),
            pltpu.VMEM((CHUNKS, ROWS, 2 * WB), BF),
            pltpu.VMEM((CHUNKS, ROWS, 2 * WB), BF),
            pltpu.VMEM((CHUNKS, ROWS, 896), BF),
            pltpu.VMEM((CHUNKS, 2, 4, 2, ROWS, WA), BF),
            pltpu.VMEM((CHUNKS, 2, 4, 2, ROWS, WB), BF),
            pltpu.VMEM((CHUNKS, 2, 8, ROWS, 512), BF),
            pltpu.VMEM((CHUNKS, 2, 2, 2, ROWS, 512), BF),
            pltpu.VMEM((CHUNKS, 2, 2, ROWS, 256), BF),
            pltpu.VMEM((CHUNKS, 2, 2, ROWS, 512), BF),
            pltpu.VMEM((CHUNKS, 2, 2, ROWS, 512), BF),
            pltpu.VMEM((CHUNKS, ROWS, 512), BF),
            pltpu.VMEM((CHUNKS, CHIPS, 2, ROWS, 512), BF),
            pltpu.VMEM((16384, 128), BF),
            pltpu.VMEM((16384, 128), BF),
            pltpu.VMEM((2, 1024, 128), BF),
            pltpu.VMEM((1024, 128), F32),
            pltpu.VMEM((128, 128), F32),
            pltpu.VMEM((8192, 512), BF),
            pltpu.VMEM((64, 8192), BF),
            pltpu.VMEM((64, 128), F32),
            pltpu.VMEM((64, 128), F32),
            pltpu.SemaphoreType.DMA((6,)),
            pltpu.SemaphoreType.DMA((KINDS, CHUNKS)),
            pltpu.SemaphoreType.DMA((KINDS, CHUNKS)),
        ],
        compiler_params=pltpu.CompilerParams(
            collective_id=0, has_side_effects=True, vmem_limit_bytes=58 * 1024 * 1024
        ),
        name="ffn_block",
    )(
        ffn_input.reshape(CHIPS, 2, 64, 512),
        w_gate_up,
        w_down,
        stream,
        attn_gain.reshape(1, 8192),
        w_query.reshape(16384, 128),
        w_kv.reshape(16384, 128),
        cache_kv.reshape(2, 1024, 128),
        cache_len,
    )
    return mixed, attended.reshape(64, 1, 2, 128)


def solution(mesh):
    in_specs = (
        P(None, ("seq", "tensor")),
        P(None, ("seq", "tensor"), "pipe"),
        P("pipe", ("seq", "tensor")),
        P("pipe", ("seq", "tensor")),
        P(),
        P(None, "tensor", "seq", None),
        P(None, None, "tensor", None),
        P("pipe", None, None, "tensor", None),
        P("pipe"),
    )
    out_specs = (P("pipe", ("seq", "tensor")), P("pipe", "tensor", "seq", None))
    return jax.shard_map(ffn_block, mesh=mesh, in_specs=in_specs, out_specs=out_specs, check_vma=False)
```

```python
import math

import jax
import jax.numpy as jnp
from jax import lax
from jax.experimental import pallas as pl
from jax.experimental.pallas import tpu as pltpu
from jax.sharding import PartitionSpec as P

norm_eps = 1e-05
rope_theta = 500000.0
MESH = pl.DeviceIdType.MESH
BF = jnp.bfloat16
F32 = jnp.float32

CHUNKS = 4
ROWS = 16
CHIPS = 8
OFFSETS = [(a, b) for a in range(2) for b in range(4)][1:]
WA, WB = 512, 384
KINDS = 13
(CORE, A1, B1, A2, B2, AG, AF, Z, ZH, ZF, XH, G, GF) = range(KINDS)
ORDER = (
    "a0", "a1", "b0", "a2", "b1", "r0", "a3", "b2", "c0", "b3", "w0",
    "c1", "j0", "w1", "c2", "j1", "w2", "k0", "c3", "j2", "w3", "e0",
    "k1", "j3", "w4", "e1", "k2", "q0", "w5", "e2", "k3", "q1", "w6",
    "e3", "g0", "q2", "w7", "g1", "q3", "h0", "g2", "i0", "h1", "g3",
    "i1", "h2", "i2", "h3", "i3", "t0",
)


def wait_bytes(ref, sem):
    pltpu.make_async_copy(ref, ref, sem).wait()


def ffn_kernel(
    x_hbm,
    wgu_hbm,
    wd_hbm,
    stream_ref,
    gain_ref,
    wq_hbm,
    wkv_hbm,
    cache_hbm,
    len_ref,
    mixed_ref,
    attended_ref,
    x_v,
    wgu_v,
    wd_v,
    core_send,
    core_recv,
    a_send,
    b_send,
    a_recv,
    b_recv,
    a_send2,
    a_recv2,
    b_own2,
    b_send2,
    b_recv2,
    hid_own,
    hid_all,
    z_send,
    z_recv,
    zh_recv,
    zf_send,
    zf_recv,
    xh_recv,
    full_all,
    wq_v,
    wkv_v,
    cache_v,
    wide_w,
    spread,
    w_all,
    normed,
    cosine,
    sine,
    load_sem,
    send_sem,
    recv_sem,
):
    p = lax.axis_index("pipe")
    s = lax.axis_index("seq")
    t = lax.axis_index("tensor")
    xh, z = p // 8, p % 8
    y, core = t // 2, t % 2
    sibling = (p, s, y * 2 + 1 - core)
    seq_peer = (p, 1 - s, t)
    x_peer = ((1 - xh) * 8 + z, s, t)

    loads = [
        pltpu.make_async_copy(src, dst, load_sem.at[i])
        for i, (src, dst) in enumerate(
            (
                (x_hbm, x_v),
                (wgu_hbm, wgu_v),
                (wd_hbm, wd_v),
                (wq_hbm, wq_v),
                (wkv_hbm, wkv_v),
                (cache_hbm, cache_v),
            )
        )
    ]
    loads[0].start()
    loads[1].start()

    def y_peer(dy):
        y2 = (y + dy) % 4
        return y2, (p, s, y2 * 2 + core)

    def group_peer(da, dy):
        return (p, (s + da) % 2, (y + dy) % 4 * 2 + core)

    def z_peer(dz):
        z2 = (z + dz) % 8
        return z2, (xh * 8 + z2, s, t)

    def cross_peer(dz):
        return ((1 - xh) * 8 + (z + dz) % 8, s, t)

    barrier = pltpu.get_barrier_semaphore()
    everyone = [sibling, x_peer]
    everyone += [group_peer(*o) for o in OFFSETS]
    everyone += [z_peer(dz)[1] for dz in (1, 2, 3, 5, 6, 7)]
    everyone += [cross_peer(sign) for sign in (1, -1)]
    for peer in everyone:
        pl.semaphore_signal(barrier, inc=1, device_id=peer, device_id_type=MESH)

    def send(src, dst, kind, c, peer):
        pltpu.make_async_remote_copy(
            src_ref=src,
            dst_ref=dst,
            send_sem=send_sem.at[kind, c],
            recv_sem=recv_sem.at[kind, c],
            device_id=peer,
            device_id_type=MESH,
        ).start()

    def arrivals(kind, c):
        return {
            CORE: core_recv.at[c],
            A1: a_recv.at[c],
            B1: b_recv.at[c],
            A2: a_recv2.at[c],
            B2: b_recv2.at[c],
            AG: hid_all.at[c, 0:7, 0],
            AF: hid_all.at[c, :, 0],
            Z: z_recv.at[c],
            ZH: zh_recv.at[c],
            ZF: zf_recv.at[c],
            XH: xh_recv.at[c],
            G: full_all.at[c, 0:7, 0],
            GF: full_all.at[c, :, 0],
        }[kind]

    def arrived(kind, c):
        wait_bytes(arrivals(kind, c), recv_sem.at[kind, c])

    def sent(kind, c):
        wait_bytes(arrivals(kind, c), send_sem.at[kind, c])

    def gate_up(rows, c):
        left = x_v[:, rows, pl.ds(c * ROWS, ROWS), :].reshape(CHIPS * ROWS, 512)
        return [
            jnp.dot(left, wgu_v[e], preferred_element_type=F32).reshape(CHIPS, ROWS, 896)
            for e in range(2)
        ]

    def stage_a(c):
        for e, part in enumerate(gate_up(1 - core, c)):
            core_send[c, :, :, e * 896 : (e + 1) * 896] = part.astype(BF)
        send(core_send.at[c], core_recv.at[c], CORE, c, sibling)

    def stage_b(c):
        parts = gate_up(core, c)
        arrived(CORE, c)
        for e, part in enumerate(parts):
            total = part + core_recv[c, :, :, e * 896 : (e + 1) * 896].astype(F32)
            total = total.astype(BF).reshape(2, 4, ROWS, 896)
            a_send[c, :, :, :, e * WA : (e + 1) * WA] = total[..., :WA]
            b_send[c, :, :, :, e * WB : (e + 1) * WB] = total[..., WA:]
        send(a_send.at[c, 1 - s], a_recv.at[c], A1, c, seq_peer)
        for dy in range(1, 4):
            y2, peer = y_peer(dy)
            send(b_send.at[c, :, y2], b_recv.at[c, dy - 1], B1, c, peer)

    def stage_c(c):
        arrived(A1, c)
        a_send2[c] = (a_send[c, s].astype(F32) + a_recv[c].astype(F32)).astype(BF)
        for dy in range(1, 4):
            y2, peer = y_peer(dy)
            send(a_send2.at[c, y2], a_recv2.at[c, dy - 1], A2, c, peer)
        arrived(B1, c)

        def total(a):
            value = b_send[c, a, y].astype(F32)
            for j in range(3):
                value = value + b_recv[c, j, a].astype(F32)
            return value

        b_send2[c] = total(1 - s).astype(BF)
        send(b_send2.at[c], b_recv2.at[c], B2, c, seq_peer)
        b_own2[c] = total(s)

    def stage_j(c):
        def swiglu(total, width):
            return (jax.nn.silu(total[:, :width]) * total[:, width:]).astype(BF)

        arrived(A2, c)
        total = a_send2[c, y].astype(F32)
        for j in range(3):
            total = total + a_recv2[c, j].astype(F32)
        hidden = swiglu(total, WA)
        hid_own[c, :, :WA] = hidden
        arrived(B2, c)
        hid_own[c, :, WA:] = swiglu(b_own2[c] + b_recv2[c].astype(F32), WB)
        k = s * 4 + y
        hid_all[c, k, core] = hid_own[c]
        for o in OFFSETS:
            send(hid_own.at[c], hid_all.at[c, k, core], AG, c, group_peer(*o))

    def stage_k(c):
        arrived(AG, c)
        send(hid_all.at[c, :, core], hid_all.at[c, :, core], AF, c, sibling)

    def stage_e(c):
        arrived(AF, c)
        out = jnp.dot(hid_all[c].reshape(256, 896), wd_v[...], preferred_element_type=F32)
        z_send[c] = out.astype(BF).reshape(2, 8, ROWS, 512)
        send(z_send.at[c, 1 - xh, z], xh_recv.at[c], XH, c, x_peer)
        for way, sign in enumerate((1, -1)):
            for hop in (1, 2):
                z2, _ = z_peer(sign * (hop + 1))
                _, peer = z_peer(sign * hop)
                send(z_send.at[c, :, z2], z_recv.at[c, way, hop - 1], Z, c, peer)
            z2, _ = z_peer(4)
            _, peer = z_peer(sign * 3)
            half = pl.ds(way * 256, 256)
            send(z_send.at[c, :, z2, :, half], zh_recv.at[c, way], ZH, c, peer)

    def stage_q(c):
        arrived(Z, c)
        arrived(ZH, c)
        for way, sign in enumerate((1, -1)):
            z2, peer = z_peer(sign)
            for h in range(2):
                cols = slice(h * 256, (h + 1) * 256)
                total = z_send[c, :, z2, :, cols].astype(F32)
                for hop in range(2):
                    total = total + z_recv[c, way, hop, :, :, cols].astype(F32)
                if h == way:
                    total = total + zh_recv[c, way].astype(F32)
                zf_send[c, way, :, :, cols] = total.astype(BF)
            send(zf_send.at[c, way, xh], zf_recv.at[c, way, 0], ZF, c, peer)
            send(zf_send.at[c, way, 1 - xh], zf_recv.at[c, way, 1], ZF, c, cross_peer(sign))

    def stage_g(c):
        arrived(XH, c)
        arrived(ZF, c)
        rows = slice(c * ROWS, (c + 1) * ROWS)
        ffn_out = z_send[c, xh, z].astype(F32) + xh_recv[c].astype(F32)
        for way in range(2):
            for side in range(2):
                ffn_out = ffn_out + zf_recv[c, way, side].astype(F32)
        mixed = (stream_ref[rows, :].astype(F32) + ffn_out).astype(BF)
        mixed_ref[rows, :] = mixed
        full_all[c, s * 4 + y, core] = mixed
        for o in OFFSETS:
            send(mixed_ref.at[rows], full_all.at[c, s * 4 + y, core], G, c, group_peer(*o))

    def stage_h(c):
        arrived(G, c)
        send(full_all.at[c, :, core], full_all.at[c, :, core], GF, c, sibling)

    def stage_i(c):
        arrived(GF, c)
        rows = slice(c * ROWS, (c + 1) * ROWS)
        squares = jnp.zeros((ROWS, 1), F32)
        for m in range(16):
            wide = full_all[c, m // 2, m % 2].astype(F32)
            squares = squares + jnp.sum(wide * wide, axis=1, keepdims=True)
        scale = lax.rsqrt(squares * (1.0 / 8192) + norm_eps)
        for m in range(16):
            cols = slice(m * 512, (m + 1) * 512)
            wide = full_all[c, m // 2, m % 2].astype(F32)
            normed[rows, cols] = (wide * scale * gain_ref[:, cols]).astype(BF)

    def stage_w(n):
        if n == 0:
            loads[3].wait()
            loads[4].wait()
        for which, source in enumerate((wq_v, wkv_v)):
            for part in range(2):
                at = n * 1024 + part * 512
                wide_w[...] = source[2 * at : 2 * at + 1024, :].astype(F32)
                for e in range(2):
                    cols = slice((2 * which + e) * 128, (2 * which + e + 1) * 128)
                    w_all[at : at + 512, cols] = wide_w[pl.ds(e, 512, stride=2), :].astype(BF)

    def stage_r(_):
        lane = lax.broadcasted_iota(jnp.int32, (64, 128), 1)
        half = lax.rem(lane, 64)
        inv_freq = jnp.exp(half.astype(F32) * (-2.0 * math.log(rope_theta) / 128))
        row = lax.broadcasted_iota(jnp.int32, (64, 128), 0)
        angles = (len_ref[0] + row).astype(F32) * inv_freq
        cosine[...] = jnp.cos(angles)
        sine[...] = jnp.where(lane < 64, -1.0, 1.0) * jnp.sin(angles)

    def stage_t(_):
        def step(i, total):
            cols = pl.ds(pl.multiple_of(i * 1024, 1024), 1024)
            return total + jnp.dot(
                normed[:, cols], w_all[cols, :], preferred_element_type=F32
            )

        total = lax.fori_loop(0, 8, step, jnp.zeros((64, 512), F32))

        def rotated(value):
            return (value * cosine[...] + pltpu.roll(value, 64, 1) * sine[...]).astype(BF)

        queries = jnp.concatenate([rotated(total[:, :128]), rotated(total[:, 128:256])], axis=0)
        k_new = rotated(total[:, 256:384])
        v_new = total[:, 384:].astype(BF)
        loads[5].wait()
        head_scale = 128 ** (-0.5)
        dims = (((1,), (1,)), ((), ()))
        cache_scores = (
            lax.dot_general(queries, cache_v[0], dims, preferred_element_type=F32) * head_scale
        )
        own_scores = lax.dot_general(queries, k_new, dims, preferred_element_type=F32) * head_scale
        spot = lax.broadcasted_iota(jnp.int32, (128, 1024), 1)
        cache_scores = jnp.where(spot < len_ref[0], cache_scores, -1e30)
        row = lax.rem(lax.broadcasted_iota(jnp.int32, (128, 64), 0), 64)
        spot = lax.broadcasted_iota(jnp.int32, (128, 64), 1)
        own_scores = jnp.where(spot <= row, own_scores, -1e30)
        row_max = jnp.maximum(
            jnp.max(cache_scores, axis=1, keepdims=True), jnp.max(own_scores, axis=1, keepdims=True)
        )
        cache_exp = jnp.exp(cache_scores - row_max)
        own_exp = jnp.exp(own_scores - row_max)
        denominator = jnp.sum(cache_exp, axis=1, keepdims=True) + jnp.sum(
            own_exp, axis=1, keepdims=True
        )
        cache_w = (cache_exp / denominator).astype(BF)
        own_w = (own_exp / denominator).astype(BF)
        result = jnp.dot(cache_w, cache_v[1], preferred_element_type=F32)
        result = result + jnp.dot(own_w, v_new, preferred_element_type=F32)
        for g in range(2):
            spread[pl.ds(g, 64, stride=2), :] = result[g * 64 : (g + 1) * 64]
        attended_ref[...] = spread[...].astype(BF)

    loads[0].wait()
    loads[1].wait()
    for load in loads[2:]:
        load.start()
    pl.semaphore_wait(barrier, len(everyone))
    stages = dict(
        a=stage_a,
        b=stage_b,
        c=stage_c,
        j=stage_j,
        k=stage_k,
        e=stage_e,
        q=stage_q,
        g=stage_g,
        h=stage_h,
        i=stage_i,
        w=stage_w,
        r=stage_r,
        t=stage_t,
    )
    waited = False
    for step in ORDER:
        if step[0] == "e" and not waited:
            loads[2].wait()
            waited = True
        stages[step[0]](int(step[1]))

    for c in range(CHUNKS):
        for kind in range(KINDS):
            sent(kind, c)


def hand_over(mixed_in, attended_in, mixed_out, attended_out):
    mixed_out[...] = mixed_in[...]
    attended_out[...] = attended_in[...]


def ffn_block(ffn_input, w_gate_up, w_down, stream, attn_gain, w_query, w_kv, cache_kv, cache_len):
    vmem = pl.BlockSpec(memory_space=pltpu.VMEM)
    hbm = pl.BlockSpec(memory_space=pl.ANY)
    smem = pl.BlockSpec(memory_space=pltpu.SMEM)
    mixed, attended = pl.pallas_call(
        ffn_kernel,
        out_shape=(
            jax.ShapeDtypeStruct((64, 512), BF),
            jax.ShapeDtypeStruct((128, 128), BF),
        ),
        in_specs=[hbm, hbm, hbm, vmem, vmem, hbm, hbm, hbm, smem],
        out_specs=(vmem, vmem),
        scratch_shapes=[
            pltpu.VMEM((CHIPS, 2, 64, 512), BF),
            pltpu.VMEM((2, 512, 896), BF),
            pltpu.VMEM((896, 512), BF),
            pltpu.VMEM((CHUNKS, CHIPS, ROWS, 1792), BF),
            pltpu.VMEM((CHUNKS, CHIPS, ROWS, 1792), BF),
            pltpu.VMEM((CHUNKS, 2, 4, ROWS, 2 * WA), BF),
            pltpu.VMEM((CHUNKS, 2, 4, ROWS, 2 * WB), BF),
            pltpu.VMEM((CHUNKS, 4, ROWS, 2 * WA), BF),
            pltpu.VMEM((CHUNKS, 3, 2, ROWS, 2 * WB), BF),
            pltpu.VMEM((CHUNKS, 4, ROWS, 2 * WA), BF),
            pltpu.VMEM((CHUNKS, 3, ROWS, 2 * WA), BF),
            pltpu.VMEM((CHUNKS, ROWS, 2 * WB), F32),
            pltpu.VMEM((CHUNKS, ROWS, 2 * WB), BF),
            pltpu.VMEM((CHUNKS, ROWS, 2 * WB), BF),
            pltpu.VMEM((CHUNKS, ROWS, 896), BF),
            pltpu.VMEM((CHUNKS, CHIPS, 2, ROWS, 896), BF),
            pltpu.VMEM((CHUNKS, 2, 8, ROWS, 512), BF),
            pltpu.VMEM((CHUNKS, 2, 2, 2, ROWS, 512), BF),
            pltpu.VMEM((CHUNKS, 2, 2, ROWS, 256), BF),
            pltpu.VMEM((CHUNKS, 2, 2, ROWS, 512), BF),
            pltpu.VMEM((CHUNKS, 2, 2, ROWS, 512), BF),
            pltpu.VMEM((CHUNKS, ROWS, 512), BF),
            pltpu.VMEM((CHUNKS, CHIPS, 2, ROWS, 512), BF),
            pltpu.VMEM((16384, 128), BF),
            pltpu.VMEM((16384, 128), BF),
            pltpu.VMEM((2, 1024, 128), BF),
            pltpu.VMEM((1024, 128), F32),
            pltpu.VMEM((128, 128), F32),
            pltpu.VMEM((8192, 512), BF),
            pltpu.VMEM((64, 8192), BF),
            pltpu.VMEM((64, 128), F32),
            pltpu.VMEM((64, 128), F32),
            pltpu.SemaphoreType.DMA((6,)),
            pltpu.SemaphoreType.DMA((KINDS, CHUNKS)),
            pltpu.SemaphoreType.DMA((KINDS, CHUNKS)),
        ],
        compiler_params=pltpu.CompilerParams(
            collective_id=0, has_side_effects=True, vmem_limit_bytes=58 * 1024 * 1024
        ),
        name="ffn_block",
    )(
        ffn_input.reshape(CHIPS, 2, 64, 512),
        w_gate_up,
        w_down,
        stream,
        attn_gain.reshape(1, 8192),
        w_query.reshape(16384, 128),
        w_kv.reshape(16384, 128),
        cache_kv.reshape(2, 1024, 128),
        cache_len,
    )
    mixed, attended = pl.pallas_call(
        hand_over,
        out_shape=(
            jax.ShapeDtypeStruct((64, 512), BF),
            jax.ShapeDtypeStruct((128, 128), BF),
        ),
        in_specs=[vmem, vmem],
        out_specs=(vmem, vmem),
        name="hand_over",
    )(mixed, attended)
    return mixed, attended.reshape(64, 1, 2, 128)


def solution(mesh):
    in_specs = (
        P(None, ("seq", "tensor")),
        P(None, ("seq", "tensor"), "pipe"),
        P("pipe", ("seq", "tensor")),
        P("pipe", ("seq", "tensor")),
        P(),
        P(None, "tensor", "seq", None),
        P(None, None, "tensor", None),
        P("pipe", None, None, "tensor", None),
        P("pipe"),
    )
    out_specs = (P("pipe", ("seq", "tensor")), P("pipe", "tensor", "seq", None))
    return jax.shard_map(ffn_block, mesh=mesh, in_specs=in_specs, out_specs=out_specs, check_vma=False)
```

```python
import math

import jax
import jax.numpy as jnp
from jax import lax
from jax.experimental import pallas as pl
from jax.experimental.pallas import tpu as pltpu
from jax.sharding import PartitionSpec as P

norm_eps = 1e-05
rope_theta = 500000.0
MESH = pl.DeviceIdType.MESH
BF = jnp.bfloat16
F32 = jnp.float32

CHUNKS = 4
ROWS = 16
CHIPS = 8
OFFSETS = ((1, 2), (0, 2), (1, 1), (1, 3), (0, 1), (0, 3), (1, 0))
WA, WB = 512, 384
KINDS = 13
(CORE, A1, B1, A2, B2, AG, AF, Z, ZH, ZF, XH, G, GF) = range(KINDS)
ORDER = (
    "a0", "a1", "b0", "a2", "b1", "r0", "a3", "b2", "c0", "b3", "w0",
    "c1", "j0", "w1", "c2", "j1", "w2", "k0", "c3", "j2", "w3", "e0",
    "k1", "j3", "w4", "e1", "k2", "q0", "w5", "e2", "k3", "q1", "w6",
    "e3", "g0", "q2", "w7", "g1", "q3", "h0", "g2", "i0", "h1", "g3",
    "i1", "h2", "i2", "s0", "h3", "u0", "i3", "t0", "s1",
)


def wait_bytes(ref, sem):
    pltpu.make_async_copy(ref, ref, sem).wait()


def ffn_kernel(
    x_hbm,
    wgu_hbm,
    wd_hbm,
    stream_ref,
    gain_ref,
    wq_hbm,
    wkv_hbm,
    cache_hbm,
    len_ref,
    mixed_ref,
    attended_ref,
    x_v,
    wgu_v,
    wd_v,
    core_send,
    core_recv,
    a_send,
    b_send,
    a_recv,
    b_recv,
    a_send2,
    a_recv2,
    b_own2,
    b_send2,
    b_recv2,
    hid_own,
    hid_all,
    z_send,
    z_recv,
    zh_recv,
    zf_send,
    zf_recv,
    xh_recv,
    full_all,
    wq_v,
    wkv_v,
    cache_v,
    wide_w,
    spread,
    w_all,
    normed,
    cosine,
    sine,
    scales,
    projected,
    load_sem,
    send_sem,
    recv_sem,
):
    p = lax.axis_index("pipe")
    s = lax.axis_index("seq")
    t = lax.axis_index("tensor")
    xh, z = p // 8, p % 8
    y, core = t // 2, t % 2
    sibling = (p, s, y * 2 + 1 - core)
    seq_peer = (p, 1 - s, t)
    x_peer = ((1 - xh) * 8 + z, s, t)

    loads = [
        pltpu.make_async_copy(src, dst, load_sem.at[i])
        for i, (src, dst) in enumerate(
            (
                (x_hbm, x_v),
                (wgu_hbm, wgu_v),
                (wd_hbm, wd_v),
                (wq_hbm, wq_v),
                (wkv_hbm, wkv_v),
                (cache_hbm, cache_v),
            )
        )
    ]
    loads[0].start()
    loads[1].start()

    def y_peer(dy):
        y2 = (y + dy) % 4
        return y2, (p, s, y2 * 2 + core)

    def group_peer(da, dy):
        return (p, (s + da) % 2, (y + dy) % 4 * 2 + core)

    def z_peer(dz):
        z2 = (z + dz) % 8
        return z2, (xh * 8 + z2, s, t)

    def cross_peer(dz):
        return ((1 - xh) * 8 + (z + dz) % 8, s, t)

    barrier = pltpu.get_barrier_semaphore()
    everyone = [sibling, x_peer]
    everyone += [group_peer(*o) for o in OFFSETS]
    everyone += [z_peer(dz)[1] for dz in (1, 2, 3, 5, 6, 7)]
    everyone += [cross_peer(sign) for sign in (1, -1)]
    for peer in everyone:
        pl.semaphore_signal(barrier, inc=1, device_id=peer, device_id_type=MESH)

    def send(src, dst, kind, c, peer):
        pltpu.make_async_remote_copy(
            src_ref=src,
            dst_ref=dst,
            send_sem=send_sem.at[kind, c],
            recv_sem=recv_sem.at[kind, c],
            device_id=peer,
            device_id_type=MESH,
        ).start()

    def arrivals(kind, c):
        return {
            CORE: core_recv.at[c],
            A1: a_recv.at[c],
            B1: b_recv.at[c],
            A2: a_recv2.at[c],
            B2: b_recv2.at[c],
            AG: hid_all.at[c, 0:7, 0],
            AF: hid_all.at[c, :, 0],
            Z: z_recv.at[c],
            ZH: zh_recv.at[c],
            ZF: zf_recv.at[c],
            XH: xh_recv.at[c],
            G: full_all.at[c, 0:7, 0],
            GF: full_all.at[c, :, 0],
        }[kind]

    def arrived(kind, c):
        wait_bytes(arrivals(kind, c), recv_sem.at[kind, c])

    def sent(kind, c):
        wait_bytes(arrivals(kind, c), send_sem.at[kind, c])

    def gate_up(rows, c):
        left = x_v[:, rows, pl.ds(c * ROWS, ROWS), :].reshape(CHIPS * ROWS, 512)
        return [
            jnp.dot(left, wgu_v[e], preferred_element_type=F32).reshape(CHIPS, ROWS, 896)
            for e in range(2)
        ]

    def stage_a(c):
        for e, part in enumerate(gate_up(1 - core, c)):
            core_send[c, :, :, e * 896 : (e + 1) * 896] = part.astype(BF)
        if c == 0:
            pl.semaphore_wait(barrier, len(everyone))
        send(core_send.at[c], core_recv.at[c], CORE, c, sibling)

    def stage_b(c):
        parts = gate_up(core, c)
        arrived(CORE, c)
        for e, part in enumerate(parts):
            total = part + core_recv[c, :, :, e * 896 : (e + 1) * 896].astype(F32)
            total = total.astype(BF).reshape(2, 4, ROWS, 896)
            a_send[c, :, :, :, e * WA : (e + 1) * WA] = total[..., :WA]
            b_send[c, :, :, :, e * WB : (e + 1) * WB] = total[..., WA:]
        send(a_send.at[c, 1 - s], a_recv.at[c], A1, c, seq_peer)
        for dy in (2, 1, 3):
            y2, peer = y_peer(dy)
            send(b_send.at[c, :, y2], b_recv.at[c, dy - 1], B1, c, peer)

    def stage_c(c):
        arrived(A1, c)
        a_send2[c] = (a_send[c, s].astype(F32) + a_recv[c].astype(F32)).astype(BF)
        for dy in (2, 1, 3):
            y2, peer = y_peer(dy)
            send(a_send2.at[c, y2], a_recv2.at[c, dy - 1], A2, c, peer)
        arrived(B1, c)

        def total(a):
            value = b_send[c, a, y].astype(F32)
            for j in range(3):
                value = value + b_recv[c, j, a].astype(F32)
            return value

        b_send2[c] = total(1 - s).astype(BF)
        send(b_send2.at[c], b_recv2.at[c], B2, c, seq_peer)
        b_own2[c] = total(s)

    def stage_j(c):
        def swiglu(total, width):
            return (jax.nn.silu(total[:, :width]) * total[:, width:]).astype(BF)

        arrived(A2, c)
        total = a_send2[c, y].astype(F32)
        for j in range(3):
            total = total + a_recv2[c, j].astype(F32)
        hidden = swiglu(total, WA)
        hid_own[c, :, :WA] = hidden
        arrived(B2, c)
        hid_own[c, :, WA:] = swiglu(b_own2[c] + b_recv2[c].astype(F32), WB)
        k = s * 4 + y
        hid_all[c, k, core] = hid_own[c]
        for o in OFFSETS:
            send(hid_own.at[c], hid_all.at[c, k, core], AG, c, group_peer(*o))

    def stage_k(c):
        arrived(AG, c)
        send(hid_all.at[c, :, core], hid_all.at[c, :, core], AF, c, sibling)

    def stage_e(c):
        arrived(AF, c)
        out = jnp.dot(hid_all[c].reshape(256, 896), wd_v[...], preferred_element_type=F32)
        z_send[c] = out.astype(BF).reshape(2, 8, ROWS, 512)
        for way, sign in enumerate((1, -1)):
            z2, _ = z_peer(4)
            half = pl.ds(way * 256, 256)
            send(z_send.at[c, :, z2, :, half], zh_recv.at[c, way], ZH, c, z_peer(sign * 3)[1])
        for hop in (2, 1):
            for way, sign in enumerate((1, -1)):
                z2, _ = z_peer(sign * (hop + 1))
                _, peer = z_peer(sign * hop)
                send(z_send.at[c, :, z2], z_recv.at[c, way, hop - 1], Z, c, peer)
        send(z_send.at[c, 1 - xh, z], xh_recv.at[c], XH, c, x_peer)

    def stage_q(c):
        arrived(Z, c)
        arrived(ZH, c)
        for way, sign in enumerate((1, -1)):
            z2, peer = z_peer(sign)
            for h in range(2):
                cols = slice(h * 256, (h + 1) * 256)
                total = z_send[c, :, z2, :, cols].astype(F32)
                for hop in range(2):
                    total = total + z_recv[c, way, hop, :, :, cols].astype(F32)
                if h == way:
                    total = total + zh_recv[c, way].astype(F32)
                zf_send[c, way, :, :, cols] = total.astype(BF)
            send(zf_send.at[c, way, xh], zf_recv.at[c, way, 0], ZF, c, peer)
            send(zf_send.at[c, way, 1 - xh], zf_recv.at[c, way, 1], ZF, c, cross_peer(sign))

    def stage_g(c):
        arrived(XH, c)
        arrived(ZF, c)
        rows = slice(c * ROWS, (c + 1) * ROWS)
        ffn_out = z_send[c, xh, z].astype(F32) + xh_recv[c].astype(F32)
        for way in range(2):
            for side in range(2):
                ffn_out = ffn_out + zf_recv[c, way, side].astype(F32)
        mixed = (stream_ref[rows, :].astype(F32) + ffn_out).astype(BF)
        mixed_ref[rows, :] = mixed
        full_all[c, s * 4 + y, core] = mixed
        for o in OFFSETS:
            send(mixed_ref.at[rows], full_all.at[c, s * 4 + y, core], G, c, group_peer(*o))

    def gained(c, which):
        rows = slice(c * ROWS, (c + 1) * ROWS)
        squares = jnp.zeros((ROWS, 1), F32)
        for k in range(CHIPS):
            wide = full_all[c, k, which].astype(F32)
            gain = gain_ref[:, pl.ds(pl.multiple_of((k * 2 + which) * 512, 512), 512)]
            squares = squares + jnp.sum(wide * wide, axis=1, keepdims=True)
            normed[which, rows, k * 512 : (k + 1) * 512] = (wide * gain).astype(BF)
        return squares

    def stage_h(c):
        arrived(G, c)
        send(full_all.at[c, :, core], full_all.at[c, :, core], GF, c, sibling)
        rows = slice(c * ROWS, (c + 1) * ROWS)
        scales[rows, :] = jnp.broadcast_to(gained(c, core), (ROWS, 128))

    def stage_i(c):
        arrived(GF, c)
        rows = slice(c * ROWS, (c + 1) * ROWS)
        squares = scales[rows, :] + gained(c, 1 - core)
        scales[rows, :] = lax.rsqrt(squares * (1.0 / 8192) + norm_eps)

    def stage_w(n):
        if n == 0:
            loads[3].wait()
            loads[4].wait()
        for which, source in enumerate((wq_v, wkv_v)):
            for part in range(2):
                at = n * 1024 + part * 512
                wide_w[...] = source[2 * at : 2 * at + 1024, :].astype(F32)
                for e in range(2):
                    cols = slice((2 * which + e) * 128, (2 * which + e + 1) * 128)
                    w_all[part, n * 512 : n * 512 + 512, cols] = wide_w[pl.ds(e, 512, stride=2), :].astype(BF)

    def stage_r(_):
        lane = lax.broadcasted_iota(jnp.int32, (64, 128), 1)
        half = lax.rem(lane, 64)
        inv_freq = jnp.exp(half.astype(F32) * (-2.0 * math.log(rope_theta) / 128))
        row = lax.broadcasted_iota(jnp.int32, (64, 128), 0)
        angles = (len_ref[0] + row).astype(F32) * inv_freq
        cosine[...] = jnp.cos(angles)
        sine[...] = jnp.where(lane < 64, -1.0, 1.0) * jnp.sin(angles)

    def project(which, total):
        def step(i, total):
            cols = pl.ds(pl.multiple_of(i * 1024, 1024), 1024)
            return total + jnp.dot(
                normed[which, :, cols], w_all[which, cols, :], preferred_element_type=F32
            )

        return lax.fori_loop(0, 4, step, total)

    def stage_u(_):
        projected[...] = project(core, jnp.zeros((64, 512), F32))

    def stage_s(n):
        for c in range(CHUNKS):
            for kind in range(KINDS):
                if (n == 0) == (c < CHUNKS - 1 or kind not in (G, GF)):
                    sent(kind, c)

    def stage_t(_):
        total = project(1 - core, projected[...]) * scales[:, :1]

        def rotated(value):
            return (value * cosine[...] + pltpu.roll(value, 64, 1) * sine[...]).astype(BF)

        queries = jnp.concatenate([rotated(total[:, :128]), rotated(total[:, 128:256])], axis=0)
        k_new = rotated(total[:, 256:384])
        v_new = total[:, 384:].astype(BF)
        loads[5].wait()
        head_scale = 128 ** (-0.5)
        dims = (((1,), (1,)), ((), ()))
        cache_scores = (
            lax.dot_general(queries, cache_v[0], dims, preferred_element_type=F32) * head_scale
        )
        own_scores = lax.dot_general(queries, k_new, dims, preferred_element_type=F32) * head_scale
        spot = lax.broadcasted_iota(jnp.int32, (128, 1024), 1)
        cache_scores = jnp.where(spot < len_ref[0], cache_scores, -1e30)
        row = lax.rem(lax.broadcasted_iota(jnp.int32, (128, 64), 0), 64)
        spot = lax.broadcasted_iota(jnp.int32, (128, 64), 1)
        own_scores = jnp.where(spot <= row, own_scores, -1e30)
        row_max = jnp.maximum(
            jnp.max(cache_scores, axis=1, keepdims=True), jnp.max(own_scores, axis=1, keepdims=True)
        )
        cache_exp = jnp.exp(cache_scores - row_max)
        own_exp = jnp.exp(own_scores - row_max)
        denominator = jnp.sum(cache_exp, axis=1, keepdims=True) + jnp.sum(
            own_exp, axis=1, keepdims=True
        )
        cache_w = (cache_exp / denominator).astype(BF)
        own_w = (own_exp / denominator).astype(BF)
        result = jnp.dot(cache_w, cache_v[1], preferred_element_type=F32)
        result = result + jnp.dot(own_w, v_new, preferred_element_type=F32)
        for g in range(2):
            spread[pl.ds(g, 64, stride=2), :] = result[g * 64 : (g + 1) * 64]
        attended_ref[...] = spread[...].astype(BF)

    loads[0].wait()
    loads[1].wait()
    for load in loads[2:]:
        load.start()
    stages = dict(
        a=stage_a,
        b=stage_b,
        c=stage_c,
        j=stage_j,
        k=stage_k,
        e=stage_e,
        q=stage_q,
        g=stage_g,
        h=stage_h,
        i=stage_i,
        w=stage_w,
        r=stage_r,
        u=stage_u,
        s=stage_s,
        t=stage_t,
    )
    waited = False
    for step in ORDER:
        if step[0] == "e" and not waited:
            loads[2].wait()
            waited = True
        stages[step[0]](int(step[1]))


def hand_over(mixed_in, attended_in, mixed_out, attended_out):
    mixed_out[...] = mixed_in[...]
    attended_out[...] = attended_in[...]


def ffn_block(ffn_input, w_gate_up, w_down, stream, attn_gain, w_query, w_kv, cache_kv, cache_len):
    vmem = pl.BlockSpec(memory_space=pltpu.VMEM)
    hbm = pl.BlockSpec(memory_space=pl.ANY)
    smem = pl.BlockSpec(memory_space=pltpu.SMEM)
    mixed, attended = pl.pallas_call(
        ffn_kernel,
        out_shape=(
            jax.ShapeDtypeStruct((64, 512), BF),
            jax.ShapeDtypeStruct((128, 128), BF),
        ),
        in_specs=[hbm, hbm, hbm, vmem, vmem, hbm, hbm, hbm, smem],
        out_specs=(vmem, vmem),
        scratch_shapes=[
            pltpu.VMEM((CHIPS, 2, 64, 512), BF),
            pltpu.VMEM((2, 512, 896), BF),
            pltpu.VMEM((896, 512), BF),
            pltpu.VMEM((CHUNKS, CHIPS, ROWS, 1792), BF),
            pltpu.VMEM((CHUNKS, CHIPS, ROWS, 1792), BF),
            pltpu.VMEM((CHUNKS, 2, 4, ROWS, 2 * WA), BF),
            pltpu.VMEM((CHUNKS, 2, 4, ROWS, 2 * WB), BF),
            pltpu.VMEM((CHUNKS, 4, ROWS, 2 * WA), BF),
            pltpu.VMEM((CHUNKS, 3, 2, ROWS, 2 * WB), BF),
            pltpu.VMEM((CHUNKS, 4, ROWS, 2 * WA), BF),
            pltpu.VMEM((CHUNKS, 3, ROWS, 2 * WA), BF),
            pltpu.VMEM((CHUNKS, ROWS, 2 * WB), F32),
            pltpu.VMEM((CHUNKS, ROWS, 2 * WB), BF),
            pltpu.VMEM((CHUNKS, ROWS, 2 * WB), BF),
            pltpu.VMEM((CHUNKS, ROWS, 896), BF),
            pltpu.VMEM((CHUNKS, CHIPS, 2, ROWS, 896), BF),
            pltpu.VMEM((CHUNKS, 2, 8, ROWS, 512), BF),
            pltpu.VMEM((CHUNKS, 2, 2, 2, ROWS, 512), BF),
            pltpu.VMEM((CHUNKS, 2, 2, ROWS, 256), BF),
            pltpu.VMEM((CHUNKS, 2, 2, ROWS, 512), BF),
            pltpu.VMEM((CHUNKS, 2, 2, ROWS, 512), BF),
            pltpu.VMEM((CHUNKS, ROWS, 512), BF),
            pltpu.VMEM((CHUNKS, CHIPS, 2, ROWS, 512), BF),
            pltpu.VMEM((16384, 128), BF),
            pltpu.VMEM((16384, 128), BF),
            pltpu.VMEM((2, 1024, 128), BF),
            pltpu.VMEM((1024, 128), F32),
            pltpu.VMEM((128, 128), F32),
            pltpu.VMEM((2, 4096, 512), BF),
            pltpu.VMEM((2, 64, 4096), BF),
            pltpu.VMEM((64, 128), F32),
            pltpu.VMEM((64, 128), F32),
            pltpu.VMEM((64, 128), F32),
            pltpu.VMEM((64, 512), F32),
            pltpu.SemaphoreType.DMA((6,)),
            pltpu.SemaphoreType.DMA((KINDS, CHUNKS)),
            pltpu.SemaphoreType.DMA((KINDS, CHUNKS)),
        ],
        compiler_params=pltpu.CompilerParams(
            collective_id=0, has_side_effects=True, vmem_limit_bytes=58 * 1024 * 1024
        ),
        name="ffn_block",
    )(
        ffn_input.reshape(CHIPS, 2, 64, 512),
        w_gate_up,
        w_down,
        stream,
        attn_gain.reshape(1, 8192),
        w_query.reshape(16384, 128),
        w_kv.reshape(16384, 128),
        cache_kv.reshape(2, 1024, 128),
        cache_len,
    )
    mixed, attended = pl.pallas_call(
        hand_over,
        out_shape=(
            jax.ShapeDtypeStruct((64, 512), BF),
            jax.ShapeDtypeStruct((128, 128), BF),
        ),
        in_specs=[vmem, vmem],
        out_specs=(vmem, vmem),
        name="hand_over",
    )(mixed, attended)
    return mixed, attended.reshape(64, 1, 2, 128)


def solution(mesh):
    in_specs = (
        P(None, ("seq", "tensor")),
        P(None, ("seq", "tensor"), "pipe"),
        P("pipe", ("seq", "tensor")),
        P("pipe", ("seq", "tensor")),
        P(),
        P(None, "tensor", "seq", None),
        P(None, None, "tensor", None),
        P("pipe", None, None, "tensor", None),
        P("pipe"),
    )
    out_specs = (P("pipe", ("seq", "tensor")), P("pipe", "tensor", "seq", None))
    return jax.shard_map(ffn_block, mesh=mesh, in_specs=in_specs, out_specs=out_specs, check_vma=False)
```

```python
import math

import jax
import jax.numpy as jnp
from jax import lax
from jax.experimental import pallas as pl
from jax.experimental.pallas import tpu as pltpu
from jax.sharding import PartitionSpec as P

norm_eps = 1e-05
rope_theta = 500000.0
MESH = pl.DeviceIdType.MESH
BF = jnp.bfloat16
F32 = jnp.float32

CHUNKS = 4
ROWS = 16
CHIPS = 8
OFFSETS = ((1, 2), (0, 2), (1, 1), (1, 3), (0, 1), (0, 3), (1, 0))
WA, WB = 512, 384
KINDS = 13
(CORE, A1, B1, A2, B2, AG, AF, Z, ZH, ZF, XH, G, GF) = range(KINDS)
ORDER = (
    "a0", "a1", "b0", "a2", "b1", "r0", "a3", "b2", "c0", "b3", "w0",
    "c1", "j0", "w1", "c2", "j1", "w2", "k0", "c3", "j2", "w3", "e0",
    "k1", "j3", "w4", "e1", "k2", "q0", "w5", "e2", "k3", "q1", "w6",
    "e3", "g0", "q2", "w7", "g1", "q3", "h0", "g2", "i0", "h1", "g3",
    "i1", "h2", "i2", "s0", "h3", "u0", "i3", "t0", "s1",
)


def wait_bytes(ref, sem):
    pltpu.make_async_copy(ref, ref, sem).wait()


def ffn_kernel(
    x_hbm,
    wgu_hbm,
    wd_hbm,
    stream_hbm,
    gain_hbm,
    wq_hbm,
    wkv_hbm,
    cache_hbm,
    len_ref,
    mixed_ref,
    attended_ref,
    x_v,
    wgu_v,
    wd_v,
    core_send,
    core_recv,
    a_send,
    b_send,
    a_recv,
    b_recv,
    a_send2,
    a_recv2,
    b_own2,
    b_send2,
    b_recv2,
    hid_own,
    hid_all,
    z_send,
    z_recv,
    zh_recv,
    zf_send,
    zf_recv,
    xh_recv,
    full_all,
    wq_v,
    wkv_v,
    cache_v,
    wide_w,
    spread,
    w_all,
    normed,
    stream_ref,
    gain_ref,
    cosine,
    sine,
    scales,
    projected,
    load_sem,
    send_sem,
    recv_sem,
):
    p = lax.axis_index("pipe")
    s = lax.axis_index("seq")
    t = lax.axis_index("tensor")
    xh, z = p // 8, p % 8
    y, core = t // 2, t % 2
    sibling = (p, s, y * 2 + 1 - core)
    seq_peer = (p, 1 - s, t)
    x_peer = ((1 - xh) * 8 + z, s, t)

    loads = [
        pltpu.make_async_copy(src, dst, load_sem.at[i])
        for i, (src, dst) in enumerate(
            (
                (x_hbm.at[:, :, 0:ROWS], x_v.at[:, :, 0:ROWS]),
                (wgu_hbm.at[0], wgu_v.at[0]),
                (wgu_hbm.at[1], wgu_v.at[1]),
                (x_hbm.at[:, :, ROWS:], x_v.at[:, :, ROWS:]),
                (wd_hbm, wd_v),
                (wq_hbm, wq_v),
                (wkv_hbm, wkv_v),
                (cache_hbm, cache_v),
                (stream_hbm, stream_ref),
                (gain_hbm, gain_ref),
            )
        )
    ]
    for load in loads[:4]:
        load.start()

    def y_peer(dy):
        y2 = (y + dy) % 4
        return y2, (p, s, y2 * 2 + core)

    def group_peer(da, dy):
        return (p, (s + da) % 2, (y + dy) % 4 * 2 + core)

    def z_peer(dz):
        z2 = (z + dz) % 8
        return z2, (xh * 8 + z2, s, t)

    def cross_peer(dz):
        return ((1 - xh) * 8 + (z + dz) % 8, s, t)

    barrier = pltpu.get_barrier_semaphore()
    everyone = [sibling, x_peer]
    everyone += [group_peer(*o) for o in OFFSETS]
    everyone += [z_peer(dz)[1] for dz in (1, 2, 3, 5, 6, 7)]
    everyone += [cross_peer(sign) for sign in (1, -1)]
    for peer in everyone:
        pl.semaphore_signal(barrier, inc=1, device_id=peer, device_id_type=MESH)

    def send(src, dst, kind, c, peer):
        pltpu.make_async_remote_copy(
            src_ref=src,
            dst_ref=dst,
            send_sem=send_sem.at[kind, c],
            recv_sem=recv_sem.at[kind, c],
            device_id=peer,
            device_id_type=MESH,
        ).start()

    def arrivals(kind, c):
        return {
            CORE: core_recv.at[c],
            A1: a_recv.at[c],
            B1: b_recv.at[c],
            A2: a_recv2.at[c],
            B2: b_recv2.at[c],
            AG: hid_all.at[c, 0:7, 0],
            AF: hid_all.at[c, :, 0],
            Z: z_recv.at[c],
            ZH: zh_recv.at[c],
            ZF: zf_recv.at[c],
            XH: xh_recv.at[c],
            G: full_all.at[c, 0:7, 0],
            GF: full_all.at[c, :, 0],
        }[kind]

    def arrived(kind, c):
        wait_bytes(arrivals(kind, c), recv_sem.at[kind, c])

    def sent(kind, c):
        wait_bytes(arrivals(kind, c), send_sem.at[kind, c])

    def gate_up(rows, c, e):
        left = x_v[:, rows, pl.ds(c * ROWS, ROWS), :].reshape(CHIPS * ROWS, 512)
        return jnp.dot(left, wgu_v[e], preferred_element_type=F32).reshape(CHIPS, ROWS, 896)

    def stage_a(c):
        for e in range(2):
            if c == 0:
                if e == 0:
                    loads[0].wait()
                loads[1 + e].wait()
            part = gate_up(1 - core, c, e)
            core_send[c, :, :, e * 896 : (e + 1) * 896] = part.astype(BF)
        if c == 0:
            pl.semaphore_wait(barrier, len(everyone))
            for load in loads[4:]:
                load.start()
        send(core_send.at[c], core_recv.at[c], CORE, c, sibling)

    def stage_b(c):
        parts = [gate_up(core, c, e) for e in range(2)]
        arrived(CORE, c)
        for e, part in enumerate(parts):
            total = part + core_recv[c, :, :, e * 896 : (e + 1) * 896].astype(F32)
            total = total.astype(BF).reshape(2, 4, ROWS, 896)
            a_send[c, :, :, :, e * WA : (e + 1) * WA] = total[..., :WA]
            b_send[c, :, :, :, e * WB : (e + 1) * WB] = total[..., WA:]
        send(a_send.at[c, 1 - s], a_recv.at[c], A1, c, seq_peer)
        for dy in (2, 1, 3):
            y2, peer = y_peer(dy)
            send(b_send.at[c, :, y2], b_recv.at[c, dy - 1], B1, c, peer)

    def stage_c(c):
        arrived(A1, c)
        a_send2[c] = (a_send[c, s].astype(F32) + a_recv[c].astype(F32)).astype(BF)
        for dy in (2, 1, 3):
            y2, peer = y_peer(dy)
            send(a_send2.at[c, y2], a_recv2.at[c, dy - 1], A2, c, peer)
        arrived(B1, c)

        def total(a):
            value = b_send[c, a, y].astype(F32)
            for j in range(3):
                value = value + b_recv[c, j, a].astype(F32)
            return value

        b_send2[c] = total(1 - s).astype(BF)
        send(b_send2.at[c], b_recv2.at[c], B2, c, seq_peer)
        b_own2[c] = total(s)

    def stage_j(c):
        def swiglu(total, width):
            return (jax.nn.silu(total[:, :width]) * total[:, width:]).astype(BF)

        arrived(A2, c)
        total = a_send2[c, y].astype(F32)
        for j in range(3):
            total = total + a_recv2[c, j].astype(F32)
        hidden = swiglu(total, WA)
        hid_own[c, :, :WA] = hidden
        arrived(B2, c)
        hid_own[c, :, WA:] = swiglu(b_own2[c] + b_recv2[c].astype(F32), WB)
        k = s * 4 + y
        hid_all[c, k, core] = hid_own[c]
        for o in OFFSETS:
            send(hid_own.at[c], hid_all.at[c, k, core], AG, c, group_peer(*o))

    def stage_k(c):
        arrived(AG, c)
        send(hid_all.at[c, :, core], hid_all.at[c, :, core], AF, c, sibling)

    def stage_e(c):
        arrived(AF, c)
        out = jnp.dot(hid_all[c].reshape(256, 896), wd_v[...], preferred_element_type=F32)
        z_send[c] = out.astype(BF).reshape(2, 8, ROWS, 512)
        for way, sign in enumerate((1, -1)):
            z2, _ = z_peer(4)
            half = pl.ds(way * 256, 256)
            send(z_send.at[c, :, z2, :, half], zh_recv.at[c, way], ZH, c, z_peer(sign * 3)[1])
        for hop in (2, 1):
            for way, sign in enumerate((1, -1)):
                z2, _ = z_peer(sign * (hop + 1))
                _, peer = z_peer(sign * hop)
                send(z_send.at[c, :, z2], z_recv.at[c, way, hop - 1], Z, c, peer)
        send(z_send.at[c, 1 - xh, z], xh_recv.at[c], XH, c, x_peer)

    def stage_q(c):
        arrived(Z, c)
        arrived(ZH, c)
        for way, sign in enumerate((1, -1)):
            z2, peer = z_peer(sign)
            for h in range(2):
                cols = slice(h * 256, (h + 1) * 256)
                total = z_send[c, :, z2, :, cols].astype(F32)
                for hop in range(2):
                    total = total + z_recv[c, way, hop, :, :, cols].astype(F32)
                if h == way:
                    total = total + zh_recv[c, way].astype(F32)
                zf_send[c, way, :, :, cols] = total.astype(BF)
            send(zf_send.at[c, way, xh], zf_recv.at[c, way, 0], ZF, c, peer)
            send(zf_send.at[c, way, 1 - xh], zf_recv.at[c, way, 1], ZF, c, cross_peer(sign))

    def stage_g(c):
        arrived(XH, c)
        arrived(ZF, c)
        rows = slice(c * ROWS, (c + 1) * ROWS)
        ffn_out = z_send[c, xh, z].astype(F32) + xh_recv[c].astype(F32)
        for way in range(2):
            for side in range(2):
                ffn_out = ffn_out + zf_recv[c, way, side].astype(F32)
        mixed = (stream_ref[rows, :].astype(F32) + ffn_out).astype(BF)
        mixed_ref[rows, :] = mixed
        full_all[c, s * 4 + y, core] = mixed
        for o in OFFSETS:
            send(mixed_ref.at[rows], full_all.at[c, s * 4 + y, core], G, c, group_peer(*o))

    def gained(c, which):
        rows = slice(c * ROWS, (c + 1) * ROWS)

        def block(k, squares):
            wide = full_all[c, k, which].astype(F32)
            gain = gain_ref[:, pl.ds(pl.multiple_of((k * 2 + which) * 512, 512), 512)]
            cols = pl.ds(pl.multiple_of(k * 512, 512), 512)
            normed[which, rows, cols] = (wide * gain).astype(BF)
            return squares + wide * wide

        squares = lax.fori_loop(0, CHIPS, block, jnp.zeros((ROWS, 512), F32))
        return jnp.sum(squares, axis=1, keepdims=True)

    def stage_h(c):
        arrived(G, c)
        send(full_all.at[c, :, core], full_all.at[c, :, core], GF, c, sibling)
        rows = slice(c * ROWS, (c + 1) * ROWS)
        scales[rows, :] = jnp.broadcast_to(gained(c, core), (ROWS, 128))

    def stage_i(c):
        arrived(GF, c)
        rows = slice(c * ROWS, (c + 1) * ROWS)
        squares = scales[rows, :] + gained(c, 1 - core)
        scales[rows, :] = lax.rsqrt(squares * (1.0 / 8192) + norm_eps)

    def stage_w(n):
        if n == 0:
            loads[5].wait()
            loads[6].wait()

        def piece(i, _):
            part, at = i // 4, i % 4 * 128
            rows = pl.ds(pl.multiple_of(n * 2048 + i * 256, 256), 256)
            for which, source in enumerate((wq_v, wkv_v)):
                wide_w[which] = source[rows, :].astype(F32)
                for e in range(2):
                    cols = slice((2 * which + e) * 128, (2 * which + e + 1) * 128)
                    into = pl.ds(pl.multiple_of(n * 512 + at, 128), 128)
                    w_all[part, into, cols] = wide_w[which, pl.ds(e, 128, stride=2), :].astype(BF)
            return 0

        lax.fori_loop(0, 8, piece, 0)

    def stage_r(_):
        lane = lax.broadcasted_iota(jnp.int32, (64, 128), 1)
        half = lax.rem(lane, 64)
        inv_freq = jnp.exp(half.astype(F32) * (-2.0 * math.log(rope_theta) / 128))
        row = lax.broadcasted_iota(jnp.int32, (64, 128), 0)
        angles = (len_ref[0] + row).astype(F32) * inv_freq
        cosine[...] = jnp.cos(angles)
        sine[...] = jnp.where(lane < 64, -1.0, 1.0) * jnp.sin(angles)

    def project(which, total):
        def step(i, total):
            cols = pl.ds(pl.multiple_of(i * 1024, 1024), 1024)
            return total + jnp.dot(
                normed[which, :, cols], w_all[which, cols, :], preferred_element_type=F32
            )

        return lax.fori_loop(0, 4, step, total)

    def stage_u(_):
        projected[...] = project(core, jnp.zeros((64, 512), F32))

    def stage_s(n):
        for c in range(CHUNKS):
            for kind in range(KINDS):
                if (n == 0) == (c < CHUNKS - 1 or kind not in (G, GF)):
                    sent(kind, c)

    def stage_t(_):
        total = project(1 - core, projected[...]) * scales[:, :1]

        def rotated(value):
            return (value * cosine[...] + pltpu.roll(value, 64, 1) * sine[...]).astype(BF)

        queries = jnp.concatenate([rotated(total[:, :128]), rotated(total[:, 128:256])], axis=0)
        k_new = rotated(total[:, 256:384])
        v_new = total[:, 384:].astype(BF)
        loads[7].wait()
        head_scale = 128 ** (-0.5)
        dims = (((1,), (1,)), ((), ()))
        cache_scores = (
            lax.dot_general(queries, cache_v[0], dims, preferred_element_type=F32) * head_scale
        )
        own_scores = lax.dot_general(queries, k_new, dims, preferred_element_type=F32) * head_scale
        spot = lax.broadcasted_iota(jnp.int32, (128, 1024), 1)
        cache_scores = jnp.where(spot < len_ref[0], cache_scores, -1e30)
        row = lax.rem(lax.broadcasted_iota(jnp.int32, (128, 64), 0), 64)
        spot = lax.broadcasted_iota(jnp.int32, (128, 64), 1)
        own_scores = jnp.where(spot <= row, own_scores, -1e30)
        row_max = jnp.maximum(
            jnp.max(cache_scores, axis=1, keepdims=True), jnp.max(own_scores, axis=1, keepdims=True)
        )
        cache_exp = jnp.exp(cache_scores - row_max)
        own_exp = jnp.exp(own_scores - row_max)
        denominator = jnp.sum(cache_exp, axis=1, keepdims=True) + jnp.sum(
            own_exp, axis=1, keepdims=True
        )
        inverse = 1.0 / denominator
        cache_w = (cache_exp * inverse).astype(BF)
        own_w = (own_exp * inverse).astype(BF)
        result = jnp.dot(cache_w, cache_v[1], preferred_element_type=F32)
        result = result + jnp.dot(own_w, v_new, preferred_element_type=F32)
        for g in range(2):
            spread[pl.ds(g, 64, stride=2), :] = result[g * 64 : (g + 1) * 64]
        attended_ref[...] = spread[...].astype(BF)

    stages = dict(
        a=stage_a,
        b=stage_b,
        c=stage_c,
        j=stage_j,
        k=stage_k,
        e=stage_e,
        q=stage_q,
        g=stage_g,
        h=stage_h,
        i=stage_i,
        w=stage_w,
        r=stage_r,
        u=stage_u,
        s=stage_s,
        t=stage_t,
    )
    first_use = {"a1": 3, "e0": 4, "g0": 8, "h0": 9}
    for step in ORDER:
        if step in first_use:
            loads[first_use[step]].wait()
        stages[step[0]](int(step[1]))


def hand_over(mixed_in, attended_in, mixed_out, attended_out):
    mixed_out[...] = mixed_in[...]
    attended_out[...] = attended_in[...]


def ffn_block(ffn_input, w_gate_up, w_down, stream, attn_gain, w_query, w_kv, cache_kv, cache_len):
    vmem = pl.BlockSpec(memory_space=pltpu.VMEM)
    hbm = pl.BlockSpec(memory_space=pl.ANY)
    smem = pl.BlockSpec(memory_space=pltpu.SMEM)
    mixed, attended = pl.pallas_call(
        ffn_kernel,
        out_shape=(
            jax.ShapeDtypeStruct((64, 512), BF),
            jax.ShapeDtypeStruct((128, 128), BF),
        ),
        in_specs=[hbm, hbm, hbm, hbm, hbm, hbm, hbm, hbm, smem],
        out_specs=(vmem, vmem),
        scratch_shapes=[
            pltpu.VMEM((CHIPS, 2, 64, 512), BF),
            pltpu.VMEM((2, 512, 896), BF),
            pltpu.VMEM((896, 512), BF),
            pltpu.VMEM((CHUNKS, CHIPS, ROWS, 1792), BF),
            pltpu.VMEM((CHUNKS, CHIPS, ROWS, 1792), BF),
            pltpu.VMEM((CHUNKS, 2, 4, ROWS, 2 * WA), BF),
            pltpu.VMEM((CHUNKS, 2, 4, ROWS, 2 * WB), BF),
            pltpu.VMEM((CHUNKS, 4, ROWS, 2 * WA), BF),
            pltpu.VMEM((CHUNKS, 3, 2, ROWS, 2 * WB), BF),
            pltpu.VMEM((CHUNKS, 4, ROWS, 2 * WA), BF),
            pltpu.VMEM((CHUNKS, 3, ROWS, 2 * WA), BF),
            pltpu.VMEM((CHUNKS, ROWS, 2 * WB), F32),
            pltpu.VMEM((CHUNKS, ROWS, 2 * WB), BF),
            pltpu.VMEM((CHUNKS, ROWS, 2 * WB), BF),
            pltpu.VMEM((CHUNKS, ROWS, 896), BF),
            pltpu.VMEM((CHUNKS, CHIPS, 2, ROWS, 896), BF),
            pltpu.VMEM((CHUNKS, 2, 8, ROWS, 512), BF),
            pltpu.VMEM((CHUNKS, 2, 2, 2, ROWS, 512), BF),
            pltpu.VMEM((CHUNKS, 2, 2, ROWS, 256), BF),
            pltpu.VMEM((CHUNKS, 2, 2, ROWS, 512), BF),
            pltpu.VMEM((CHUNKS, 2, 2, ROWS, 512), BF),
            pltpu.VMEM((CHUNKS, ROWS, 512), BF),
            pltpu.VMEM((CHUNKS, CHIPS, 2, ROWS, 512), BF),
            pltpu.VMEM((16384, 128), BF),
            pltpu.VMEM((16384, 128), BF),
            pltpu.VMEM((2, 1024, 128), BF),
            pltpu.VMEM((2, 256, 128), F32),
            pltpu.VMEM((128, 128), F32),
            pltpu.VMEM((2, 4096, 512), BF),
            pltpu.VMEM((2, 64, 4096), BF),
            pltpu.VMEM((64, 512), BF),
            pltpu.VMEM((1, 8192), F32),
            pltpu.VMEM((64, 128), F32),
            pltpu.VMEM((64, 128), F32),
            pltpu.VMEM((64, 128), F32),
            pltpu.VMEM((64, 512), F32),
            pltpu.SemaphoreType.DMA((10,)),
            pltpu.SemaphoreType.DMA((KINDS, CHUNKS)),
            pltpu.SemaphoreType.DMA((KINDS, CHUNKS)),
        ],
        compiler_params=pltpu.CompilerParams(
            collective_id=0, has_side_effects=True, vmem_limit_bytes=58 * 1024 * 1024
        ),
        name="ffn_block",
    )(
        ffn_input.reshape(CHIPS, 2, 64, 512),
        w_gate_up,
        w_down,
        stream,
        attn_gain.reshape(1, 8192),
        w_query.reshape(16384, 128),
        w_kv.reshape(16384, 128),
        cache_kv.reshape(2, 1024, 128),
        cache_len,
    )
    mixed, attended = pl.pallas_call(
        hand_over,
        out_shape=(
            jax.ShapeDtypeStruct((64, 512), BF),
            jax.ShapeDtypeStruct((128, 128), BF),
        ),
        in_specs=[vmem, vmem],
        out_specs=(vmem, vmem),
        name="hand_over",
    )(mixed, attended)
    return mixed, attended.reshape(64, 1, 2, 128)


def solution(mesh):
    in_specs = (
        P(None, ("seq", "tensor")),
        P(None, ("seq", "tensor"), "pipe"),
        P("pipe", ("seq", "tensor")),
        P("pipe", ("seq", "tensor")),
        P(),
        P(None, "tensor", "seq", None),
        P(None, None, "tensor", None),
        P("pipe", None, None, "tensor", None),
        P("pipe"),
    )
    out_specs = (P("pipe", ("seq", "tensor")), P("pipe", "tensor", "seq", None))
    return jax.shard_map(ffn_block, mesh=mesh, in_specs=in_specs, out_specs=out_specs, check_vma=False)
```
